256 devices in a mesh: key: 64 (over z, y, core), partner: 4 (over x).
Axes of the slice: x: 4, y: 4, z: 8, core: 2. Of those that a mesh axis runs over, the one named last changes fastest.
Arguments:
- embeddings: bfloat16 [65536, 1024], P('key'), may hold values from -1 to 1
- sources: int32 [64, 256, 1], P('key', 'partner'), may hold values from 0 to 63; in each aligned block of 64 rows (0 to 63, 64 to 127, ..., all dimensions but the last counted through in order) at most 2 rows name the same one
- blocks: int32 [64, 256], P('key', 'partner'), may hold values from 0 to 63
Outputs:
- log_density: float32 [65536], P('key')
- neighbour_mean: bfloat16 [65536, 1024], P('key')
The draws below stay inside these ranges and needn't reach their ends.
Inputs may be any that keep to these rules, and one draw needn't show every extreme that they name: `sources`: among the 64 slots of one device (aligned blocks of slots) no key range is named more than 2 times, and some key range exactly 2 times.
All inputs are finite; a program needn't handle non-finite values.
Results may differ from the reference program's by a relative error of at most 0.0034.
Values may be sent and summed in bfloat16 or wider, within the bound.
No kernel may reach another device: no remote copies, remote signals or barrier semaphores. Data moves between devices by JAX's collectives and lax.ppermute only.
A program may use at most 64 MiB of HBM per device.

```python
import math
import jax
import jax.numpy as jnp
import numpy as np
from jax import lax

D = 1024
SLAB = 1024
BR = 16
CAP = 2
NBD = 64
KEYS = 64
PARTNER_SLOTS = 256


def draw_embeddings(key, part):
    key = jax.random.fold_in(key, 11)
    key_a, key_b, key_c, key_d, key_e, key_f, key_g = jax.random.split(key, 7)
    count = KEYS * SLAB
    group_total = 8
    span = min(32, D // group_total)
    centres = jax.random.normal(key_a, (group_total, D), jnp.float32) / math.sqrt(D)
    favourite = jax.random.randint(key_b, (KEYS,), 0, group_total)
    picked = jax.random.randint(key_c, (count,), 0, 2)
    spread = jax.random.randint(key_d, (count,), 0, group_total)
    range_of_row = jnp.arange(count, dtype=jnp.int32) // SLAB
    member = jnp.where(picked == 0, favourite[range_of_row], spread)
    coefs = jax.random.normal(key_e, (count, span), jnp.float32)
    noise = jax.random.normal(key_f, (count, D), jnp.float32)
    tiled = jnp.tile(coefs, (1, group_total))
    owner = jnp.arange(group_total * span, dtype=jnp.int32) // span
    local = jnp.where(owner[None, :] == member[:, None], tiled, 0.0) / math.sqrt(span)
    local = jnp.pad(local, ((0, 0), (0, D - group_total * span)))
    order = jax.random.permutation(key_g, D)
    local = local[:, order]
    rows = math.sqrt(0.72) * centres[member] + math.sqrt(0.25) * local + math.sqrt(0.03) * noise / math.sqrt(D)
    return jnp.clip(rows, -1.0, 1.0).astype(jnp.bfloat16)


def touch_ends(entries, key, smallest, top_value):
    index_at = [jax.random.randint(jax.random.fold_in(key, axis), (), 0, length) for axis, length in enumerate(entries.shape)]
    main_axis = entries.shape.index(max(entries.shape))
    neighbour = index_at[:main_axis] + [(index_at[main_axis] + 1) % entries.shape[main_axis]] + index_at[main_axis + 1:]
    return entries.at[tuple(index_at)].set(smallest).at[tuple(neighbour)].set(top_value)


def shared_out(rng, own, number, rows, number_of, top, reach, lean):
    ranking = jax.random.permutation(rng, number_of)
    crowded, common = load_shares(number_of, rows * top, reach, lean, True), load_shares(number_of, rows * top, reach, lean, False)
    places = jnp.arange(number_of)

    def named(sizes, rotation):
        used = int((sizes > 0).sum())
        fixed = max(1, used // 4)
        passed = fixed + (places - fixed + rotation * (used - fixed)) % max(1, number_of - fixed)
        return jnp.zeros((number_of,), jnp.int32).at[ranking[jnp.where(places < fixed, places, passed)]].set(jnp.asarray(sizes, jnp.int32))

    sizes = jnp.where(number % 4 == 0, named(crowded, number // 4), named(common, number - number // 4 - 1))
    mixed = jax.random.permutation(jax.random.fold_in(own, 3), number_of)
    giver, sink = mixed[0:number_of // 2 * 2:2], mixed[1:number_of // 2 * 2:2]
    slack = jnp.minimum(sizes[giver] - 1, reach - sizes[sink]) // 2
    slack = jnp.where((giver == ranking[0]) | (sink == ranking[0]) | (sizes[sink] == 0), 0, jnp.maximum(slack, 0))
    passed = jax.random.randint(jax.random.fold_in(own, 4), (number_of // 2,), 0, 1 << 20) % (slack + 1)
    sizes = sizes.at[giver].add(-passed).at[sink].add(passed)
    members = jnp.searchsorted(jnp.cumsum(sizes), jnp.arange(rows * top), side="right").astype(jnp.int32)
    table = members.reshape(top, rows).T
    table = table[jax.random.permutation(jax.random.fold_in(own, 1), rows)]
    rotation = jax.random.randint(jax.random.fold_in(own, 2), (rows, 1), 0, top)
    return jnp.take_along_axis(table, (jnp.arange(top)[None, :] + rotation) % top, axis=1)


def load_shares(amount, total, reach, lean, full):
    portions = [(1 << 20) // math.isqrt(grade ** lean) + 1 for grade in range(1, amount + 1)]
    largest = reach if full else min(reach, max(-(-total // amount), total * portions[0] // sum(portions)))
    least = 1 if total - largest >= amount - 1 else 0
    holding, surplus = [largest] + [least] * (amount - 1), total - largest - least * (amount - 1)
    while surplus > 0:
        free = [i for i in range(1, amount) if holding[i] < largest] or [i for i in range(1, amount) if holding[i] < reach]
        pool, budget = sum([portions[i] for i in free]), surplus
        for i in free:
            addition = min(reach - holding[i], max(1, budget * portions[i] // pool), surplus)
            holding[i] = holding[i] + addition
            surplus = surplus - addition
    return np.array(holding)


def setup_inputs(seed: int = 0) -> dict:
    keys = jax.random.split(jax.random.key(seed), 4)
    embeddings = draw_embeddings(jax.random.fold_in(keys[3], 71), 0)
    sources_keys = jax.random.split(jax.random.fold_in(keys[1], 1), KEYS * PARTNER_SLOTS // NBD)
    sources_turns = jax.random.permutation(jax.random.fold_in(keys[1], 3), KEYS * PARTNER_SLOTS // NBD)
    sources = jax.vmap(lambda own, number: shared_out(jax.random.fold_in(keys[1], 2), own, number, NBD, KEYS, 1, CAP, 2))(sources_keys, sources_turns).reshape((KEYS, PARTNER_SLOTS, 1))
    blocks = touch_ends(jax.random.randint(keys[2], (KEYS, PARTNER_SLOTS), 0, SLAB // BR), jax.random.fold_in(keys[2], 1), 0, (SLAB // BR) - 1).astype(jnp.int32)
    return {"embeddings": embeddings, "sources": sources, "blocks": blocks}


TEMP = 0.05


def reference(embeddings, sources, blocks):
    nblock = SLAB // BR
    slab_all = embeddings.reshape(KEYS, nblock, BR, D)

    def one_key(carry, k):
        acc_w, acc_k = carry
        own = slab_all[k].reshape(SLAB, D)
        src = sources[k, :, 0]
        blk = blocks[k]
        flat = slab_all[src, blk].reshape(PARTNER_SLOTS * BR, D)
        cosine = jnp.dot(own, flat.T, preferred_element_type=jnp.float32)
        weight = jnp.exp((cosine - 1.0) / TEMP)
        rounded = weight.astype(jnp.bfloat16)
        own_k = jnp.sum(weight, axis=1)
        own_w = jnp.dot(rounded, flat, preferred_element_type=jnp.float32)
        part_k = jnp.sum(weight, axis=0).astype(jnp.bfloat16)
        part_w = jnp.dot(rounded.T, own, preferred_element_type=jnp.float32).astype(jnp.bfloat16)
        part_k = lax.optimization_barrier(part_k).astype(jnp.float32).reshape(PARTNER_SLOTS, BR)
        part_w = lax.optimization_barrier(part_w).astype(jnp.float32).reshape(PARTNER_SLOTS, BR, D)
        acc_w = acc_w.at[src, blk].add(part_w)
        acc_k = acc_k.at[src, blk].add(part_k)
        acc_w = acc_w.at[k].add(own_w.reshape(nblock, BR, D))
        acc_k = acc_k.at[k].add(own_k.reshape(nblock, BR))
        return (acc_w, acc_k), None

    start = (jnp.zeros((KEYS, nblock, BR, D), jnp.float32), jnp.zeros((KEYS, nblock, BR), jnp.float32))
    (total_w, total_k), unused = lax.scan(one_key, start, jnp.arange(KEYS, dtype=jnp.int32))
    total_w = total_w.reshape(KEYS * SLAB, D)
    total_k = total_k.reshape(KEYS * SLAB)
    scale = 1.0 + total_k
    mean = ((embeddings.astype(jnp.float32) + total_w) / scale[:, None]).astype(jnp.bfloat16)
    return jnp.log(scale), mean
```

```python
import jax
import jax.numpy as jnp
from jax import lax
from jax.experimental import pallas as pl
from jax.experimental.pallas import tpu as pltpu
from jax.sharding import Mesh, PartitionSpec as P

D = 1024
SLAB = 1024
BR = 16
NBLK = SLAB // BR
NBD = 64
KEYS = 64
NZ, NY, NC, NX = 8, 4, 2, 4
PIECES = NY * NC
RP = BR // PIECES
CX = D // NX
W = RP * CX
PLANE = NX * NY * NC
TEMP = 0.05

F32, BF16 = jnp.float32, jnp.bfloat16
NT = (((1,), (1,)), ((), ()))
TN = (((0,), (0,)), ((), ()))


def pair_kernel(emb_ref, inc_ref, own_ref, ownk_ref, cred_ref, credk_ref, acc_ref):
    emb = emb_ref[...]
    for y in range(NY):
        rows = []
        for c in range(NC):
            for r in range(RP):
                rows.append(
                    jnp.concatenate(
                        [
                            inc_ref[pl.ds((x * PIECES + NC * y + c) * NBD, NBD), pl.ds(r * CX, CX)]
                            for x in range(NX)
                        ],
                        axis=1,
                    )
                )
        part = jnp.concatenate(rows, axis=0)
        cosine = lax.dot_general(emb, part, NT, preferred_element_type=F32)
        weight = jnp.exp((cosine - 1.0) * (1.0 / TEMP))
        rounded = weight.astype(BF16)
        lanes = weight[:, :128] + weight[:, 128:]
        prod = jnp.dot(rounded, part, preferred_element_type=F32)
        if y == 0:
            ownk_ref[...] = lanes
            acc_ref[...] = prod
        else:
            ownk_ref[...] += lanes
            acc_ref[...] += prod
        credk_ref[pl.ds(y, 1), :] = jnp.sum(weight, axis=0, keepdims=True)
        cred = lax.dot_general(rounded, emb, TN, preferred_element_type=F32).astype(BF16)
        for c in range(NC):
            for r in range(RP):
                at = (c * RP + r) * NBD
                for x in range(NX):
                    cred_ref[pl.ds((x * PIECES + NC * y + c) * NBD, NBD), pl.ds(r * CX, CX)] = cred[
                        at : at + NBD, x * CX : (x + 1) * CX
                    ]
    for x in range(NX):
        own_ref[x] = acc_ref[:, x * CX : (x + 1) * CX].astype(BF16)


def pair_sums(emb, inc):
    return pl.pallas_call(
        pair_kernel,
        out_shape=(
            jax.ShapeDtypeStruct((NX, SLAB, CX), BF16),
            jax.ShapeDtypeStruct((SLAB, 128), F32),
            jax.ShapeDtypeStruct((PLANE * NBD, W), BF16),
            jax.ShapeDtypeStruct((NY, NC * RP * NBD), F32),
        ),
        in_specs=[pl.BlockSpec(memory_space=pltpu.VMEM)] * 2,
        out_specs=[pl.BlockSpec(memory_space=pltpu.VMEM)] * 4,
        scratch_shapes=[pltpu.VMEM((SLAB, D), F32)],
        compiler_params=pltpu.CompilerParams(vmem_limit_bytes=48 << 20),
        cost_estimate=pl.CostEstimate(
            flops=6 * SLAB * SLAB * D, bytes_accessed=10 << 20, transcendentals=SLAB * SLAB
        ),
    )(emb, inc)


def shift(axis, by):
    n = lax.axis_size(axis)
    return [(i, (i + by) % n) for i in range(n)]


def up(a, axis):
    return lax.ppermute(a, axis, shift(axis, 1))


def down(a, axis):
    return lax.ppermute(a, axis, shift(axis, -1))


def sum_over_x(own):
    me = lax.axis_index("x")
    half = SLAB // 2
    to = lambda k: lax.dynamic_index_in_dim(own, lax.rem(me + k, NX), 0, keepdims=False)
    far, right, left, mine = to(2), to(1), to(3), to(0)
    far_up, far_down = up(far[:half], "x"), down(far[half:], "x")
    from_left = [
        up((right[:half].astype(F32) + far_up.astype(F32)).astype(BF16), "x"),
        up(right[half:], "x"),
    ]
    from_right = [
        down(left[:half], "x"),
        down((left[half:].astype(F32) + far_down.astype(F32)).astype(BF16), "x"),
    ]
    return mine.astype(F32) + (
        jnp.concatenate(from_left).astype(F32) + jnp.concatenate(from_right).astype(F32)
    )


def gather_over_x(mine):
    me = lax.axis_index("x")
    half = SLAB // 2
    parts = [mine[:half], mine[half:]]
    ups = [up(p, "x") for p in parts]
    downs = [down(p, "x") for p in parts]
    far = [up(ups[0], "x"), down(downs[1], "x")]
    out = jnp.zeros((SLAB, D), BF16)
    place = lambda out, a, row, k: lax.dynamic_update_slice(
        out, a, (row, lax.rem(me + k, NX) * CX)
    )
    out = place(out, mine, 0, 0)
    for p in range(2):
        out = place(out, ups[p], p * half, 3)
        out = place(out, downs[p], p * half, 1)
        out = place(out, far[p], p * half, 2)
    return out


def local(embeddings, sources, blocks):
    me_x = lax.axis_index("x")
    me_key = lax.axis_index(("z", "y", "c"))
    columns = lax.dynamic_slice_in_dim(embeddings, me_x * CX, CX, axis=1)
    pieces = columns.reshape(NBLK, PIECES, W).transpose(1, 0, 2).reshape(PIECES * NBLK, W)
    held = lax.all_to_all(pieces, ("y", "c"), 0, 0, tiled=True)
    table = lax.all_gather(held, "z", tiled=True)

    wanted = sources[0, :, 0] * NBLK + blocks[0]
    plane_wanted = lax.all_to_all(
        jnp.broadcast_to(jnp.pad(wanted, (0, 128 - NBD)), (PLANE, 128)),
        ("x", "y", "c"), 0, 0, tiled=True,
    )[:, :NBD].reshape(-1)
    every = jnp.arange(KEYS * NBLK, dtype=jnp.int32)
    pick = (plane_wanted[:, None] == every[None, :]).astype(BF16)
    outgoing = jnp.dot(pick, table, preferred_element_type=F32).astype(BF16)
    incoming = lax.all_to_all(outgoing, ("x", "y", "c"), 0, 0, tiled=True)

    own, own_k, credit, credit_k = pair_sums(embeddings, incoming)

    back = lax.all_to_all(credit, ("x", "y", "c"), 0, 0, tiled=True)
    spread = (every[:, None] == plane_wanted[None, :]).astype(BF16)
    dense = jnp.dot(spread, back, preferred_element_type=F32).astype(BF16)
    got = lax.psum_scatter(dense, "z", tiled=True)

    own_w = sum_over_x(own)
    per_slot = credit_k.astype(BF16).reshape(NY, NC, RP, NBD).transpose(3, 0, 1, 2).reshape(NBD, BR)
    spread_k = (every[:, None] == wanted[None, :]).astype(BF16)
    dense_k = jnp.dot(spread_k, per_slot, preferred_element_type=F32).reshape(KEYS, SLAB)
    mine = jnp.arange(KEYS, dtype=jnp.int32)[:, None] == me_key
    dense_k = dense_k + jnp.where(mine, jnp.sum(own_k, axis=1)[None, :], 0.0)
    all_k = lax.all_to_all(dense_k, ("z", "y", "c"), 0, 0, tiled=True)
    total_k = lax.psum(jnp.sum(all_k, axis=0), "x")
    scale = 1.0 + total_k

    got = lax.all_to_all(got, ("y", "c"), 0, 0, tiled=True)
    got = got.reshape(PIECES, NBLK, W).transpose(1, 0, 2).reshape(SLAB, CX)
    total_w = own_w + got.astype(F32)
    mean = ((columns.astype(F32) + total_w) / scale[:, None]).astype(BF16)
    return jnp.log(scale), gather_over_x(mean)


def solution(mesh):
    fine = Mesh(mesh.devices.reshape(NZ, NY, NC, NX), ("z", "y", "c", "x"))
    key = ("z", "y", "c")
    in_specs = (P(key, None), P(key, "x", None), P(key, "x"))
    out_specs = (P(key), P(key, None))
    return jax.shard_map(local, mesh=fine, in_specs=in_specs, out_specs=out_specs, check_vma=False)
```

```python
import jax
import jax.numpy as jnp
from jax import lax
from jax.experimental import pallas as pl
from jax.experimental.pallas import tpu as pltpu
from jax.sharding import Mesh, PartitionSpec as P

D = 1024
SLAB = 1024
BR = 16
NBLK = SLAB // BR
NBD = 64
KEYS = 64
NZ, NY, NC, NX = 8, 4, 2, 4
PIECES = NY * NC
RP = BR // PIECES
CX = D // NX
W = RP * CX
PLANE = NX * NY * NC
TEMP = 0.05

F32, BF16 = jnp.float32, jnp.bfloat16
NT = (((1,), (1,)), ((), ()))
TN = (((0,), (0,)), ((), ()))


def pair_kernel(emb_ref, inc_ref, own_ref, ownk_ref, cred_ref, credk_ref, acc_ref):
    emb = emb_ref[...]
    for y in range(NY):
        rows = []
        for c in range(NC):
            for r in range(RP):
                rows.append(
                    jnp.concatenate(
                        [
                            inc_ref[pl.ds((x * PIECES + NC * y + c) * NBD, NBD), pl.ds(r * CX, CX)]
                            for x in range(NX)
                        ],
                        axis=1,
                    )
                )
        part = jnp.concatenate(rows, axis=0)
        cosine = lax.dot_general(emb, part, NT, preferred_element_type=F32)
        weight = jnp.exp((cosine - 1.0) * (1.0 / TEMP))
        rounded = weight.astype(BF16)
        lanes = weight[:, :128] + weight[:, 128:]
        prod = jnp.dot(rounded, part, preferred_element_type=F32)
        if y == 0:
            ownk_ref[...] = lanes
            acc_ref[...] = prod
        else:
            ownk_ref[...] += lanes
            acc_ref[...] += prod
        credk_ref[pl.ds(y, 1), :] = jnp.sum(weight, axis=0, keepdims=True)
        cred = lax.dot_general(rounded, emb, TN, preferred_element_type=F32).astype(BF16)
        for c in range(NC):
            for r in range(RP):
                at = (c * RP + r) * NBD
                for x in range(NX):
                    cred_ref[pl.ds((x * PIECES + NC * y + c) * NBD, NBD), pl.ds(r * CX, CX)] = cred[
                        at : at + NBD, x * CX : (x + 1) * CX
                    ]
    for x in range(NX):
        own_ref[x] = acc_ref[:, x * CX : (x + 1) * CX].astype(BF16)


def pair_sums(emb, inc):
    return pl.pallas_call(
        pair_kernel,
        out_shape=(
            jax.ShapeDtypeStruct((NX, SLAB, CX), BF16),
            jax.ShapeDtypeStruct((SLAB, 128), F32),
            jax.ShapeDtypeStruct((PLANE * NBD, W), BF16),
            jax.ShapeDtypeStruct((NY, NC * RP * NBD), F32),
        ),
        in_specs=[pl.BlockSpec(memory_space=pltpu.VMEM)] * 2,
        out_specs=[pl.BlockSpec(memory_space=pltpu.VMEM)] * 4,
        scratch_shapes=[pltpu.VMEM((SLAB, D), F32)],
        compiler_params=pltpu.CompilerParams(vmem_limit_bytes=48 << 20),
        cost_estimate=pl.CostEstimate(
            flops=6 * SLAB * SLAB * D, bytes_accessed=10 << 20, transcendentals=SLAB * SLAB
        ),
    )(emb, inc)


def shift(axis, by):
    n = lax.axis_size(axis)
    return [(i, (i + by) % n) for i in range(n)]


def up(a, axis):
    return lax.ppermute(a, axis, shift(axis, 1))


def down(a, axis):
    return lax.ppermute(a, axis, shift(axis, -1))


def gather_over_x(mine):
    me = lax.axis_index("x")
    half = SLAB // 2
    parts = [mine[:half], mine[half:]]
    ups = [up(p, "x") for p in parts]
    downs = [down(p, "x") for p in parts]
    far = [up(ups[0], "x"), down(downs[1], "x")]
    place = lambda out, a, row, k: lax.dynamic_update_slice(
        out, a, (row, lax.rem(me + k, NX) * CX)
    )
    out = jnp.concatenate([mine] * NX, axis=1)
    for p in range(2):
        out = place(out, ups[p], p * half, 3)
        out = place(out, downs[p], p * half, 1)
        out = place(out, far[p], p * half, 2)
    return out


def pick_over_z(held, plane_wanted):
    me = lax.axis_index("z")
    rows = held.shape[0]
    half = rows // 2
    inside = jnp.arange(rows, dtype=jnp.int32)
    picked = None

    def take(picked, parts):
        at = jnp.concatenate(
            [lax.rem(me + k, NZ) * rows + inside[first : first + t.shape[0]] for k, first, t in parts]
        )
        pick = (plane_wanted[:, None] == at[None, :]).astype(BF16)
        got = jnp.dot(pick, jnp.concatenate([t for _, _, t in parts]), preferred_element_type=F32)
        return (got if picked is None else got + picked.astype(F32)).astype(BF16)

    ups = downs = [held[:half], held[half:]]
    picked = take(None, [(0, 0, held)])
    for step in range(1, NZ // 2):
        ups = [up(t, "z") for t in ups]
        downs = [down(t, "z") for t in downs]
        picked = take(
            picked,
            [(NZ - step, p * half, ups[p]) for p in range(2)]
            + [(step, p * half, downs[p]) for p in range(2)],
        )
    far = [(NZ // 2, 0, up(ups[0], "z")), (NZ // 2, half, down(downs[1], "z"))]
    return take(picked, far)


def sum_over_z(back, plane_wanted):
    me = lax.axis_index("z")
    rows = PIECES * NBLK
    half = rows // 2
    inside = jnp.arange(rows, dtype=jnp.int32)

    def table(k):
        spread = (lax.rem(me + k, NZ) * rows + inside)[:, None] == plane_wanted[None, :]
        dense = jnp.dot(spread.astype(BF16), back, preferred_element_type=F32)
        return lax.optimization_barrier(dense)

    far = NZ // 2
    first = table(far).astype(BF16)
    ups, downs = up(first[:half], "z"), down(first[half:], "z")
    for k in range(far - 1, 0, -1):
        add_up, add_down = table(k), table(NZ - k)
        if k == far - 1:
            ups = jnp.concatenate([add_up[:half] + ups.astype(F32), add_up[half:]])
            downs = jnp.concatenate([add_down[:half], add_down[half:] + downs.astype(F32)])
        else:
            ups = add_up + ups.astype(F32)
            downs = add_down + downs.astype(F32)
        ups, downs = up(ups.astype(BF16), "z"), down(downs.astype(BF16), "z")
    return (table(0) + (ups.astype(F32) + downs.astype(F32))).astype(BF16)


def local(embeddings, sources, blocks):
    me_x = lax.axis_index("x")
    me_key = lax.axis_index(("z", "y", "c"))
    columns = lax.dynamic_slice_in_dim(embeddings, me_x * CX, CX, axis=1)
    pieces = columns.reshape(NBLK, PIECES, W).transpose(1, 0, 2).reshape(PIECES * NBLK, W)
    held = lax.all_to_all(pieces, ("y", "c"), 0, 0, tiled=True)

    wanted = sources[0, :, 0] * NBLK + blocks[0]
    held, late = lax.optimization_barrier((held, wanted))
    plane_wanted = lax.all_to_all(
        jnp.broadcast_to(jnp.pad(late, (0, 128 - NBD)), (PLANE, 128)),
        ("x", "y", "c"), 0, 0, tiled=True,
    )[:, :NBD].reshape(-1)
    every = jnp.arange(KEYS * NBLK, dtype=jnp.int32)
    outgoing = pick_over_z(held, plane_wanted)
    incoming = lax.all_to_all(outgoing, ("x", "y", "c"), 0, 0, tiled=True)

    own, own_k, credit, credit_k = pair_sums(embeddings, incoming)

    back = lax.all_to_all(credit, ("x", "y", "c"), 0, 0, tiled=True)
    per_slot = credit_k.astype(BF16).reshape(NY, NC, RP, NBD).transpose(0, 1, 2, 3).reshape(BR, NBD)
    spread_k = (wanted[:, None] == every[None, :]).astype(BF16)
    dense_k = jnp.dot(per_slot, spread_k, preferred_element_type=F32)
    back, own, dense_k = lax.optimization_barrier((back, own, dense_k))
    own_w = lax.psum_scatter(own, "x", tiled=True)[0]
    got = sum_over_z(back, plane_wanted)
    all_k = lax.all_to_all(dense_k.reshape(BR, KEYS, NBLK), ("z", "y", "c"), 1, 0, tiled=True)
    got_k = jnp.sum(all_k.reshape(KEYS, BR, NBLK), axis=0).T.reshape(SLAB)
    total_k = lax.psum(got_k + jnp.sum(own_k, axis=1), "x")
    scale = 1.0 + total_k

    got, own_w, scale = lax.optimization_barrier((got, own_w, scale))
    got = lax.all_to_all(got, ("y", "c"), 0, 0, tiled=True)
    rows = jnp.arange(SLAB, dtype=jnp.int32)
    source = (rows % RP) * (SLAB // RP) + (rows % BR) // RP * NBLK + rows // BR
    got = got.reshape(PIECES * NBLK, W)
    got = jnp.concatenate([got[:, r * CX : (r + 1) * CX] for r in range(RP)])
    order = (source[:, None] == rows[None, :]).astype(BF16)
    total_w = own_w.astype(F32) + jnp.dot(order, got, preferred_element_type=F32)
    mean = ((columns.astype(F32) + total_w) / scale[:, None]).astype(BF16)
    return jnp.log(scale), gather_over_x(lax.optimization_barrier(mean))


def solution(mesh):
    fine = Mesh(mesh.devices.reshape(NZ, NY, NC, NX), ("z", "y", "c", "x"))
    key = ("z", "y", "c")
    in_specs = (P(key, None), P(key, "x", None), P(key, "x"))
    out_specs = (P(key), P(key, None))
    return jax.shard_map(local, mesh=fine, in_specs=in_specs, out_specs=out_specs, check_vma=False)
```

```python
import jax
import jax.numpy as jnp
from jax import lax
from jax.experimental import pallas as pl
from jax.experimental.pallas import tpu as pltpu
from jax.sharding import Mesh, PartitionSpec as P

D = 1024
SLAB = 1024
BR = 16
NBLK = SLAB // BR
NBD = 64
KEYS = 64
NZ, NY, NC, NX = 8, 4, 2, 4
PIECES = NY * NC
RP = BR // PIECES
CX = D // NX
W = RP * CX
PLANE = NX * NY * NC
TEMP = 0.05

F32, BF16 = jnp.float32, jnp.bfloat16
NT = (((1,), (1,)), ((), ()))
TN = (((0,), (0,)), ((), ()))


def pair_kernel(emb_ref, inc_ref, part_ref, rounded_ref, ownk_ref, cred_ref, credk_ref):
    emb = emb_ref[...]
    group = NC * RP * NBD
    for y in range(NY):
        for c in range(NC):
            for r in range(RP):
                for x in range(NX):
                    part_ref[pl.ds(y * group + (c * RP + r) * NBD, NBD), pl.ds(x * CX, CX)] = inc_ref[
                        pl.ds((x * PIECES + NC * y + c) * NBD, NBD), pl.ds(r * CX, CX)
                    ]
        part = part_ref[pl.ds(y * group, group), :]
        cosine = lax.dot_general(emb, part, NT, preferred_element_type=F32)
        weight = jnp.exp((cosine - 1.0) * (1.0 / TEMP))
        rounded = weight.astype(BF16)
        rounded_ref[:, pl.ds(y * group, group)] = rounded
        lanes = weight[:, :128] + weight[:, 128:]
        if y == 0:
            ownk_ref[...] = lanes
        else:
            ownk_ref[...] += lanes
        credk_ref[pl.ds(y, 1), :] = jnp.sum(weight, axis=0, keepdims=True)
        cred = lax.dot_general(rounded, emb, TN, preferred_element_type=F32).astype(BF16)
        for c in range(NC):
            for r in range(RP):
                at = (c * RP + r) * NBD
                for x in range(NX):
                    cred_ref[pl.ds((x * PIECES + NC * y + c) * NBD, NBD), pl.ds(r * CX, CX)] = cred[
                        at : at + NBD, x * CX : (x + 1) * CX
                    ]


def pair_weights(emb, inc):
    vmem = pl.BlockSpec(memory_space=pltpu.VMEM)
    return pl.pallas_call(
        pair_kernel,
        out_shape=(
            jax.ShapeDtypeStruct((SLAB, D), BF16),
            jax.ShapeDtypeStruct((SLAB, SLAB), BF16),
            jax.ShapeDtypeStruct((SLAB, 128), F32),
            jax.ShapeDtypeStruct((PLANE * NBD, W), BF16),
            jax.ShapeDtypeStruct((NY, NC * RP * NBD), F32),
        ),
        in_specs=[vmem] * 2,
        out_specs=[vmem] * 5,
        compiler_params=pltpu.CompilerParams(vmem_limit_bytes=20 << 20),
        cost_estimate=pl.CostEstimate(
            flops=4 * SLAB * SLAB * D, bytes_accessed=10 << 20, transcendentals=SLAB * SLAB
        ),
    )(emb, inc)


def own_kernel(rounded_ref, part_ref, own_ref):
    for x in range(NX):
        own_ref[x] = jnp.dot(
            rounded_ref[...], part_ref[:, x * CX : (x + 1) * CX], preferred_element_type=F32
        ).astype(BF16)


def own_sums(rounded, part):
    vmem = pl.BlockSpec(memory_space=pltpu.VMEM)
    return pl.pallas_call(
        own_kernel,
        out_shape=jax.ShapeDtypeStruct((NX, SLAB, CX), BF16),
        in_specs=[vmem] * 2,
        out_specs=vmem,
        compiler_params=pltpu.CompilerParams(vmem_limit_bytes=12 << 20),
        cost_estimate=pl.CostEstimate(
            flops=2 * SLAB * SLAB * D, bytes_accessed=6 << 20, transcendentals=0
        ),
    )(rounded, part)


def shift(axis, by):
    n = lax.axis_size(axis)
    return [(i, (i + by) % n) for i in range(n)]


def up(a, axis):
    return lax.ppermute(a, axis, shift(axis, 1))


def down(a, axis):
    return lax.ppermute(a, axis, shift(axis, -1))


def gather_over_x(mine):
    me = lax.axis_index("x")
    half = SLAB // 2
    parts = [mine[:half], mine[half:]]
    ups = [up(p, "x") for p in parts]
    downs = [down(p, "x") for p in parts]
    far = [up(ups[0], "x"), down(downs[1], "x")]
    place = lambda out, a, row, k: lax.dynamic_update_slice(
        out, a, (row, lax.rem(me + k, NX) * CX)
    )
    out = jnp.concatenate([mine] * NX, axis=1)
    for p in range(2):
        out = place(out, ups[p], p * half, 3)
        out = place(out, downs[p], p * half, 1)
        out = place(out, far[p], p * half, 2)
    return out


def share_in_plane(wanted):
    padded = jnp.broadcast_to(jnp.pad(wanted, (0, 128 - NBD)), (PLANE, 128))
    return lax.all_to_all(padded, ("x", "y", "c"), 0, 0, tiled=True)[:, :NBD].reshape(-1)


def pick_over_z(held, wanted):
    me = lax.axis_index("z")
    rows = held.shape[0]
    half = rows // 2
    inside = jnp.arange(rows, dtype=jnp.int32)
    picked = None

    def take(picked, parts):
        at = jnp.concatenate(
            [lax.rem(me + k, NZ) * rows + inside[first : first + t.shape[0]] for k, first, t in parts]
        )
        pick = (plane_wanted[:, None] == at[None, :]).astype(BF16)
        got = jnp.dot(pick, jnp.concatenate([t for _, _, t in parts]), preferred_element_type=F32)
        return (got if picked is None else got + picked.astype(F32)).astype(BF16)

    ups = downs = [held[:half], held[half:]]
    plane_wanted = None
    for step in range(1, NZ // 2):
        ups = [up(t, "z") for t in ups]
        downs = [down(t, "z") for t in downs]
        if step == 1:
            ups, downs, wanted = lax.optimization_barrier((ups, downs, wanted))
            plane_wanted = share_in_plane(wanted)
            picked = take(None, [(0, 0, held)])
        picked = take(
            picked,
            [(NZ - step, p * half, ups[p]) for p in range(2)]
            + [(step, p * half, downs[p]) for p in range(2)],
        )
    far = [(NZ // 2, 0, up(ups[0], "z")), (NZ // 2, half, down(downs[1], "z"))]
    return take(picked, far), plane_wanted


def sum_over_z(back, plane_wanted, later):
    me = lax.axis_index("z")
    rows = PIECES * NBLK
    half = rows // 2
    inside = jnp.arange(rows, dtype=jnp.int32)

    def table(k):
        spread = (lax.rem(me + k, NZ) * rows + inside)[:, None] == plane_wanted[None, :]
        dense = jnp.dot(spread.astype(BF16), back, preferred_element_type=F32)
        return lax.optimization_barrier(dense)

    far = NZ // 2
    first = table(far).astype(BF16)
    ups, downs = up(first[:half], "z"), down(first[half:], "z")
    for k in range(far - 1, 0, -1):
        add_up, add_down = table(k), table(NZ - k)
        if k == far - 1:
            ups = jnp.concatenate([add_up[:half] + ups.astype(F32), add_up[half:]])
            downs = jnp.concatenate([add_down[:half], add_down[half:] + downs.astype(F32)])
        else:
            ups = add_up + ups.astype(F32)
            downs = add_down + downs.astype(F32)
        if k == far - 1:
            ups, downs, later = lax.optimization_barrier((ups, downs, later))
        ups, downs = up(ups.astype(BF16), "z"), down(downs.astype(BF16), "z")
    return (table(0) + (ups.astype(F32) + downs.astype(F32))).astype(BF16), later


def local(embeddings, sources, blocks):
    me_x = lax.axis_index("x")
    me_key = lax.axis_index(("z", "y", "c"))
    columns = lax.dynamic_slice_in_dim(embeddings, me_x * CX, CX, axis=1)
    pieces = columns.reshape(NBLK, PIECES, W).transpose(1, 0, 2).reshape(PIECES * NBLK, W)
    held = lax.all_to_all(pieces, ("y", "c"), 0, 0, tiled=True)

    wanted = sources[0, :, 0] * NBLK + blocks[0]
    outgoing, plane_wanted = pick_over_z(held, wanted)
    incoming = lax.all_to_all(outgoing, ("x", "y", "c"), 0, 0, tiled=True)

    part, rounded, own_k, credit, credit_k = pair_weights(embeddings, incoming)
    back = lax.all_to_all(credit, ("x", "y", "c"), 0, 0, tiled=True)
    own = own_sums(rounded, part)
    own_w = lax.psum_scatter(own, "x", tiled=True)[0]

    per_slot = credit_k.astype(BF16).reshape(BR, NBD)
    every = jnp.arange(KEYS * NBLK, dtype=jnp.int32)
    spread_k = (wanted[:, None] == every[None, :]).astype(BF16)
    dense_k = jnp.dot(per_slot, spread_k, preferred_element_type=F32).reshape(BR, KEYS, NBLK)

    got, dense_k = sum_over_z(back, plane_wanted, dense_k)
    all_k = lax.all_to_all(dense_k, ("z", "y", "c"), 1, 0, tiled=True)
    got_k = jnp.sum(all_k.reshape(KEYS, BR, NBLK), axis=0).T.reshape(SLAB) + jnp.sum(own_k, axis=1)
    got, own_w, got_k = lax.optimization_barrier((got, own_w, got_k))
    scale = 1.0 + lax.psum(got_k, "x")
    got = lax.all_to_all(got, ("y", "c"), 0, 0, tiled=True)
    rows = jnp.arange(SLAB, dtype=jnp.int32)
    source = (rows % RP) * (SLAB // RP) + (rows % BR) // RP * NBLK + rows // BR
    got = got.reshape(PIECES * NBLK, W)
    got = jnp.concatenate([got[:, r * CX : (r + 1) * CX] for r in range(RP)])
    order = (source[:, None] == rows[None, :]).astype(BF16)
    total_w = own_w.astype(F32) + jnp.dot(order, got, preferred_element_type=F32)
    mean = ((columns.astype(F32) + total_w) / scale[:, None]).astype(BF16)
    return jnp.log(scale), gather_over_x(lax.optimization_barrier(mean))


def solution(mesh):
    fine = Mesh(mesh.devices.reshape(NZ, NY, NC, NX), ("z", "y", "c", "x"))
    key = ("z", "y", "c")
    in_specs = (P(key, None), P(key, "x", None), P(key, "x"))
    out_specs = (P(key), P(key, None))
    return jax.shard_map(local, mesh=fine, in_specs=in_specs, out_specs=out_specs, check_vma=False)
```

```python
import jax
import jax.numpy as jnp
from jax import lax
from jax.experimental import pallas as pl
from jax.experimental.pallas import tpu as pltpu
from jax.sharding import Mesh, PartitionSpec as P

D = 1024
SLAB = 1024
BR = 16
NBLK = SLAB // BR
NBD = 64
KEYS = 64
NZ, NY, NC, NX = 8, 4, 2, 4
PIECES = NY * NC
RP = BR // PIECES
CX = D // NX
W = RP * CX
PLANE = NX * NY * NC
TEMP = 0.05

F32, BF16 = jnp.float32, jnp.bfloat16
NT = (((1,), (1,)), ((), ()))
TN = (((0,), (0,)), ((), ()))


def pair_kernel(emb_ref, inc_ref, part_ref, rounded_ref, ownk_ref, cred_ref, credk_ref):
    y = pl.program_id(0)
    emb = emb_ref[...]
    for c in range(NC):
        for r in range(RP):
            for x in range(NX):
                part_ref[pl.ds((c * RP + r) * NBD, NBD), pl.ds(x * CX, CX)] = inc_ref[
                    x, c, :, pl.ds(r * CX, CX)
                ]
    cosine = lax.dot_general(emb, part_ref[...], NT, preferred_element_type=F32)
    weight = jnp.exp((cosine - 1.0) * (1.0 / TEMP))
    rounded = weight.astype(BF16)
    rounded_ref[...] = rounded
    lanes = weight[:, :128] + weight[:, 128:]

    @pl.when(y == 0)
    def _():
        ownk_ref[...] = lanes

    @pl.when(y > 0)
    def _():
        ownk_ref[...] += lanes

    credk_ref[0] = jnp.sum(weight, axis=0, keepdims=True)
    cred = lax.dot_general(rounded, emb, TN, preferred_element_type=F32).astype(BF16)
    for c in range(NC):
        for r in range(RP):
            at = (c * RP + r) * NBD
            for x in range(NX):
                cred_ref[x, c, :, pl.ds(r * CX, CX)] = cred[at : at + NBD, x * CX : (x + 1) * CX]


def pair_weights(emb, inc):
    group = NC * RP * NBD
    pieces = pl.BlockSpec((NX, NC, NBD, W), lambda y: (0, y, 0, 0))
    return pl.pallas_call(
        pair_kernel,
        grid=(NY,),
        out_shape=(
            pltpu.HBM((SLAB, D), BF16),
            pltpu.HBM((SLAB, SLAB), BF16),
            jax.ShapeDtypeStruct((SLAB, 128), F32),
            jax.ShapeDtypeStruct((NX, PIECES, NBD, W), BF16),
            jax.ShapeDtypeStruct((NY, 1, group), F32),
        ),
        in_specs=[pl.BlockSpec((SLAB, D), lambda y: (0, 0)), pieces],
        out_specs=(
            pl.BlockSpec((group, D), lambda y: (y, 0)),
            pl.BlockSpec((SLAB, group), lambda y: (0, y)),
            pl.BlockSpec((SLAB, 128), lambda y: (0, 0)),
            pieces,
            pl.BlockSpec((1, 1, group), lambda y: (y, 0, 0)),
        ),
        compiler_params=pltpu.CompilerParams(vmem_limit_bytes=16 << 20),
        cost_estimate=pl.CostEstimate(
            flops=4 * SLAB * SLAB * D, bytes_accessed=10 << 20, transcendentals=SLAB * SLAB
        ),
    )(emb, inc.reshape(NX, PIECES, NBD, W))


def own_kernel(rounded_ref, part_ref, own_ref):
    own_ref[0] = jnp.dot(rounded_ref[...], part_ref[...], preferred_element_type=F32).astype(BF16)


def own_sums(rounded, part):
    return pl.pallas_call(
        own_kernel,
        grid=(NX,),
        out_shape=pltpu.HBM((NX, SLAB, CX), BF16),
        in_specs=[
            pl.BlockSpec((SLAB, SLAB), lambda x: (0, 0)),
            pl.BlockSpec((SLAB, CX), lambda x: (0, x)),
        ],
        out_specs=pl.BlockSpec((1, SLAB, CX), lambda x: (x, 0, 0)),
        compiler_params=pltpu.CompilerParams(vmem_limit_bytes=12 << 20),
        cost_estimate=pl.CostEstimate(
            flops=2 * SLAB * SLAB * D, bytes_accessed=6 << 20, transcendentals=0
        ),
    )(*[pltpu.with_memory_space_constraint(a, pltpu.HBM) for a in (rounded, part)])


def shift(axis, by):
    n = lax.axis_size(axis)
    return [(i, (i + by) % n) for i in range(n)]


def up(a, axis):
    return lax.ppermute(a, axis, shift(axis, 1))


def down(a, axis):
    return lax.ppermute(a, axis, shift(axis, -1))


def gather_over_x(mine):
    me = lax.axis_index("x")
    half = SLAB // 2
    parts = [mine[:half], mine[half:]]
    ups = [up(p, "x") for p in parts]
    downs = [down(p, "x") for p in parts]
    far = [up(ups[0], "x"), down(downs[1], "x")]
    place = lambda out, a, row, k: lax.dynamic_update_slice(
        out, a, (row, lax.rem(me + k, NX) * CX)
    )
    out = jnp.concatenate([mine] * NX, axis=1)
    for p in range(2):
        out = place(out, ups[p], p * half, 3)
        out = place(out, downs[p], p * half, 1)
        out = place(out, far[p], p * half, 2)
    return out


def share_in_plane(wanted):
    padded = jnp.broadcast_to(jnp.pad(wanted, (0, 128 - NBD)), (PLANE, 128))
    return lax.all_to_all(padded, ("x", "y", "c"), 0, 0, tiled=True)[:, :NBD].reshape(-1)


def pick_over_z(held, wanted):
    me = lax.axis_index("z")
    rows = held.shape[0]
    half = rows // 2
    inside = jnp.arange(rows, dtype=jnp.int32)
    picked = None

    def take(picked, parts):
        at = jnp.concatenate(
            [lax.rem(me + k, NZ) * rows + inside[first : first + t.shape[0]] for k, first, t in parts]
        )
        pick = (plane_wanted[:, None] == at[None, :]).astype(BF16)
        got = jnp.dot(pick, jnp.concatenate([t for _, _, t in parts]), preferred_element_type=F32)
        return (got if picked is None else got + picked.astype(F32)).astype(BF16)

    ups, downs = up(held, "z"), down(held, "z")
    ups, downs, wanted = lax.optimization_barrier((ups, downs, wanted))
    plane_wanted = share_in_plane(wanted)
    picked = take(None, [(0, 0, held)])
    for step in range(1, NZ // 2):
        picked = take(picked, [(NZ - step, 0, ups), (step, 0, downs)])
        if step < NZ // 2 - 1:
            ups, downs = up(ups, "z"), down(downs, "z")
    far = [(NZ // 2, 0, up(ups[:half], "z")), (NZ // 2, half, down(downs[half:], "z"))]
    return take(picked, far), plane_wanted


def sum_over_z(back, plane_wanted, later):
    me = lax.axis_index("z")
    rows = PIECES * NBLK
    half = rows // 2
    inside = jnp.arange(rows, dtype=jnp.int32)

    def table(k, first, last):
        at = lax.rem(me + k, NZ) * rows + inside[first:last]
        spread = (at[:, None] == plane_wanted[None, :]).astype(BF16)
        return jnp.dot(spread, back, preferred_element_type=F32)

    far = NZ // 2
    ups = up(table(far, 0, half).astype(BF16), "z")
    downs = down(table(far, half, rows).astype(BF16), "z")
    for k in range(far - 1, 0, -1):
        if k == far - 1:
            ups, downs, later = lax.optimization_barrier((ups, downs, later))
            add_up = jnp.concatenate([ups.astype(F32), jnp.zeros((half, W), F32)])
            add_down = jnp.concatenate([jnp.zeros((half, W), F32), downs.astype(F32)])
        else:
            add_up, add_down = ups.astype(F32), downs.astype(F32)
        ups = up((table(k, 0, rows) + add_up).astype(BF16), "z")
        downs = down((table(NZ - k, 0, rows) + add_down).astype(BF16), "z")
    return (table(0, 0, rows) + (ups.astype(F32) + downs.astype(F32))).astype(BF16), later


def local(embeddings, sources, blocks):
    me_x = lax.axis_index("x")
    me_key = lax.axis_index(("z", "y", "c"))
    columns = lax.dynamic_slice_in_dim(embeddings, me_x * CX, CX, axis=1)
    pieces = columns.reshape(NBLK, PIECES, W).transpose(1, 0, 2).reshape(PIECES * NBLK, W)
    held = lax.all_to_all(pieces, ("y", "c"), 0, 0, tiled=True)

    wanted = sources[0, :, 0] * NBLK + blocks[0]
    outgoing, plane_wanted = pick_over_z(held, wanted)
    incoming = lax.all_to_all(outgoing, ("x", "y", "c"), 0, 0, tiled=True)

    part, rounded, own_k, credit, credit_k = pair_weights(embeddings, incoming)
    credit = credit.reshape(PLANE * NBD, W)
    back = lax.all_to_all(credit, ("x", "y", "c"), 0, 0, tiled=True)
    back, own = lax.optimization_barrier((back, own_sums(rounded, part)))
    own_w = lax.psum_scatter(own, "x", tiled=True)[0]

    per_slot = credit_k.astype(BF16).reshape(BR, NBD)
    every = jnp.arange(KEYS * NBLK, dtype=jnp.int32)
    spread_k = (wanted[:, None] == every[None, :]).astype(BF16)
    dense_k = jnp.dot(per_slot, spread_k, preferred_element_type=F32).reshape(BR, KEYS, NBLK)

    got, dense_k = sum_over_z(back, plane_wanted, dense_k)
    all_k = lax.all_to_all(dense_k, ("z", "y", "c"), 1, 0, tiled=True)
    got_k = jnp.sum(all_k.reshape(KEYS, BR, NBLK), axis=0).T.reshape(SLAB) + jnp.sum(own_k, axis=1)
    got, own_w, got_k = lax.optimization_barrier((got, own_w, got_k))
    scale = 1.0 + lax.psum(got_k, "x")
    got = lax.all_to_all(got, ("y", "c"), 0, 0, tiled=True)
    rows = jnp.arange(SLAB, dtype=jnp.int32)
    source = (rows % RP) * (SLAB // RP) + (rows % BR) // RP * NBLK + rows // BR
    got = got.reshape(PIECES * NBLK, W)
    got = jnp.concatenate([got[:, r * CX : (r + 1) * CX] for r in range(RP)])
    order = (source[:, None] == rows[None, :]).astype(BF16)
    total_w = own_w.astype(F32) + jnp.dot(order, got, preferred_element_type=F32)
    mean = ((columns.astype(F32) + total_w) / scale[:, None]).astype(BF16)
    return jnp.log(scale), gather_over_x(lax.optimization_barrier(mean))


def solution(mesh):
    fine = Mesh(mesh.devices.reshape(NZ, NY, NC, NX), ("z", "y", "c", "x"))
    key = ("z", "y", "c")
    in_specs = (P(key, None), P(key, "x", None), P(key, "x"))
    out_specs = (P(key), P(key, None))
    return jax.shard_map(local, mesh=fine, in_specs=in_specs, out_specs=out_specs, check_vma=False)
```

```python
import jax
import jax.numpy as jnp
from jax import lax
from jax.experimental import pallas as pl
from jax.experimental.pallas import tpu as pltpu
from jax.sharding import Mesh, PartitionSpec as P

D = 1024
SLAB = 1024
BR = 16
NBLK = SLAB // BR
NBD = 64
KEYS = 64
NZ, NY, NC, NX = 8, 4, 2, 4
PIECES = NY * NC
RP = BR // PIECES
CX = D // NX
W = CX
PLANE = NX * NY * NC
TEMP = 0.05

F32, BF16 = jnp.float32, jnp.bfloat16
NT = (((1,), (1,)), ((), ()))
TN = (((0,), (0,)), ((), ()))


def pair_kernel(emb_ref, inc_ref, part_ref, rounded_ref, ownk_ref, cred_ref, credk_ref):
    emb = emb_ref[...]
    group = 4 * NBD
    for first in range(0, PIECES * NBD, group):
        for n in range(4):
            for x in range(NX):
                part_ref[pl.ds(first + n * NBD, NBD), pl.ds(x * CX, CX)] = inc_ref[x, first // NBD + n]
        part = part_ref[pl.ds(first, group), :]
        cosine = lax.dot_general(emb, part, NT, preferred_element_type=F32)
        weight = jnp.exp((cosine - 1.0) * (1.0 / TEMP))
        rounded = weight.astype(BF16)
        rounded_ref[:, pl.ds(first, group)] = rounded
        lanes = weight[:, :128] + weight[:, 128:]
        if first == 0:
            ownk_ref[...] = lanes
        else:
            ownk_ref[...] += lanes
        credk_ref[:, pl.ds(first, group)] = jnp.sum(weight, axis=0, keepdims=True)
        cred = lax.dot_general(rounded, emb, TN, preferred_element_type=F32).astype(BF16)
        for n in range(4):
            for x in range(NX):
                cred_ref[x, first // NBD + n] = cred[n * NBD : (n + 1) * NBD, x * CX : (x + 1) * CX]


def pair_weights(emb, inc):
    rows = PIECES * NBD
    return pl.pallas_call(
        pair_kernel,
        out_shape=(
            pltpu.HBM((rows, D), BF16),
            pltpu.HBM((SLAB, rows), BF16),
            jax.ShapeDtypeStruct((SLAB, 128), F32),
            jax.ShapeDtypeStruct((NX, PIECES, NBD, W), BF16),
            jax.ShapeDtypeStruct((1, rows), F32),
        ),
        compiler_params=pltpu.CompilerParams(vmem_limit_bytes=16 << 20),
        cost_estimate=pl.CostEstimate(
            flops=4 * SLAB * rows * D, bytes_accessed=7 << 20, transcendentals=SLAB * rows
        ),
    )(emb, inc.reshape(NX, PIECES, NBD, W))


def own_kernel(rounded0_ref, part0_ref, rounded1_ref, part1_ref, own_ref):
    own = jnp.dot(rounded0_ref[...], part0_ref[...], preferred_element_type=F32)
    own += jnp.dot(rounded1_ref[...], part1_ref[...], preferred_element_type=F32)
    own_ref[0] = own.astype(BF16)


def own_sums(rounded0, part0, rounded1, part1):
    rows = PIECES * NBD
    specs = [
        pl.BlockSpec((SLAB, rows), lambda x: (0, 0)),
        pl.BlockSpec((rows, CX), lambda x: (0, x)),
    ]
    return pl.pallas_call(
        own_kernel,
        grid=(NX,),
        out_shape=pltpu.HBM((NX, SLAB, CX), BF16),
        in_specs=specs * RP,
        out_specs=pl.BlockSpec((1, SLAB, CX), lambda x: (x, 0, 0)),
        compiler_params=pltpu.CompilerParams(vmem_limit_bytes=12 << 20),
        cost_estimate=pl.CostEstimate(
            flops=2 * SLAB * SLAB * D, bytes_accessed=6 << 20, transcendentals=0
        ),
    )(*[pltpu.with_memory_space_constraint(a, pltpu.HBM) for a in (rounded0, part0, rounded1, part1)])


def shift(axis, by):
    n = lax.axis_size(axis)
    return [(i, (i + by) % n) for i in range(n)]


def up(a, axis):
    return lax.ppermute(a, axis, shift(axis, 1))


def down(a, axis):
    return lax.ppermute(a, axis, shift(axis, -1))


def gather_over_x(mine):
    me = lax.axis_index("x")
    half = SLAB // 2
    parts = [mine[:half], mine[half:]]
    ups = [up(p, "x") for p in parts]
    downs = [down(p, "x") for p in parts]
    far = [up(ups[0], "x"), down(downs[1], "x")]
    place = lambda out, a, row, k: lax.dynamic_update_slice(
        out, a, (row, lax.rem(me + k, NX) * CX)
    )
    out = jnp.concatenate([mine] * NX, axis=1)
    for p in range(2):
        out = place(out, ups[p], p * half, 3)
        out = place(out, downs[p], p * half, 1)
        out = place(out, far[p], p * half, 2)
    return out


def share_in_plane(wanted):
    padded = jnp.broadcast_to(jnp.pad(wanted, (0, 128 - NBD)), (PLANE, 128))
    return lax.all_to_all(padded, ("x", "y", "c"), 0, 0, tiled=True)[:, :NBD].reshape(-1)


def pick_over_z(held, plane_wanted):
    me = lax.axis_index("z")
    rows = held.shape[0]
    half = rows // 2
    inside = jnp.arange(rows, dtype=jnp.int32)

    def take(picked, parts):
        at = jnp.concatenate(
            [lax.rem(me + k, NZ) * rows + inside[first : first + t.shape[0]] for k, first, t in parts]
        )
        pick = (plane_wanted[:, None] == at[None, :]).astype(BF16)
        got = jnp.dot(pick, jnp.concatenate([t for _, _, t in parts]), preferred_element_type=F32)
        return (got if picked is None else got + picked.astype(F32)).astype(BF16)

    ups = downs = held
    picked = take(None, [(0, 0, held)])
    for step in range(1, NZ // 2):
        ups, downs = up(ups, "z"), down(downs, "z")
        picked = take(picked, [(NZ - step, 0, ups), (step, 0, downs)])
    far = [(NZ // 2, 0, up(ups[:half], "z")), (NZ // 2, half, down(downs[half:], "z"))]
    return take(picked, far)


def sum_over_z(back, plane_wanted, later):
    me = lax.axis_index("z")
    rows = PIECES * NBLK
    half = rows // 2
    inside = jnp.arange(rows, dtype=jnp.int32)

    def table(k, first, last):
        at = lax.rem(me + k, NZ) * rows + inside[first:last]
        spread = (at[:, None] == plane_wanted[None, :]).astype(BF16)
        return jnp.dot(spread, back, preferred_element_type=F32)

    far = NZ // 2
    ups = up(table(far, 0, half).astype(BF16), "z")
    downs = down(table(far, half, rows).astype(BF16), "z")
    for k in range(far - 1, 0, -1):
        if k == far - 1:
            ups, downs, later = lax.optimization_barrier((ups, downs, later))
            add_up = jnp.concatenate([ups.astype(F32), jnp.zeros((half, W), F32)])
            add_down = jnp.concatenate([jnp.zeros((half, W), F32), downs.astype(F32)])
        else:
            add_up, add_down = ups.astype(F32), downs.astype(F32)
        ups = up((table(k, 0, rows) + add_up).astype(BF16), "z")
        downs = down((table(NZ - k, 0, rows) + add_down).astype(BF16), "z")
    return (table(0, 0, rows) + (ups.astype(F32) + downs.astype(F32))).astype(BF16), later


def in_plane(a):
    return lax.all_to_all(a, ("x", "y", "c"), 0, 0, tiled=True)


def local(embeddings, sources, blocks):
    me_x = lax.axis_index("x")
    columns = lax.dynamic_slice_in_dim(embeddings, me_x * CX, CX, axis=1)
    pieces = columns.reshape(NBLK, PIECES, RP * W).transpose(1, 0, 2).reshape(PIECES * NBLK, RP * W)
    held = lax.all_to_all(pieces, ("y", "c"), 0, 0, tiled=True)
    table1 = lax.all_gather(held[:, W:], "z", tiled=True)

    wanted = sources[0, :, 0] * NBLK + blocks[0]
    held, late = lax.optimization_barrier((held, wanted))
    plane_wanted = share_in_plane(late)
    every = jnp.arange(KEYS * NBLK, dtype=jnp.int32)
    incoming0 = in_plane(pick_over_z(held[:, :W], plane_wanted))
    pick = (plane_wanted[:, None] == every[None, :]).astype(BF16)
    incoming1 = in_plane(jnp.dot(pick, table1, preferred_element_type=F32).astype(BF16))

    part0, rounded0, own_k0, credit0, credit_k0 = pair_weights(embeddings, incoming0)
    credit0, incoming1 = lax.optimization_barrier((credit0, incoming1))
    part1, rounded1, own_k1, credit1, credit_k1 = pair_weights(embeddings, incoming1)
    back0 = in_plane(credit0.reshape(PLANE * NBD, W))
    back0, credit1 = lax.optimization_barrier((back0, credit1))
    back1 = in_plane(credit1.reshape(PLANE * NBD, W))
    spread = (every[:, None] == plane_wanted[None, :]).astype(BF16)
    dense0 = jnp.dot(spread, back0, preferred_element_type=F32).astype(BF16)
    got0 = lax.psum_scatter(dense0, "z", tiled=True)
    back1, own = lax.optimization_barrier((back1, own_sums(rounded0, part0, rounded1, part1)))
    own_w = lax.psum_scatter(own, "x", tiled=True)[0]

    credit_k = jnp.stack([credit_k0.reshape(PIECES, NBD), credit_k1.reshape(PIECES, NBD)], axis=1)
    per_slot = credit_k.astype(BF16).reshape(BR, NBD)
    spread_k = (wanted[:, None] == every[None, :]).astype(BF16)
    dense_k = jnp.dot(per_slot, spread_k, preferred_element_type=F32).reshape(BR, KEYS, NBLK)

    got1, dense_k = sum_over_z(back1, plane_wanted, dense_k)
    all_k = lax.all_to_all(dense_k, ("z", "y", "c"), 1, 0, tiled=True)
    got_k = jnp.sum(all_k.reshape(KEYS, BR, NBLK), axis=0).T.reshape(SLAB)
    got_k = got_k + jnp.sum(own_k0 + own_k1, axis=1)
    got = jnp.concatenate([got0, got1], axis=1)
    got, got_k = lax.optimization_barrier((got, got_k))
    scale = 1.0 + lax.psum(got_k, "x")
    got = lax.all_to_all(got, ("y", "c"), 0, 0, tiled=True)
    got, own_w = lax.optimization_barrier((got, own_w))
    rows = jnp.arange(SLAB, dtype=jnp.int32)
    source = (rows % RP) * (SLAB // RP) + (rows % BR) // RP * NBLK + rows // BR
    got = jnp.concatenate([got[:, r * CX : (r + 1) * CX] for r in range(RP)])
    order = (source[:, None] == rows[None, :]).astype(BF16)
    total_w = own_w.astype(F32) + jnp.dot(order, got, preferred_element_type=F32)
    mean = ((columns.astype(F32) + total_w) / scale[:, None]).astype(BF16)
    return jnp.log(scale), gather_over_x(lax.optimization_barrier(mean))


def solution(mesh):
    fine = Mesh(mesh.devices.reshape(NZ, NY, NC, NX), ("z", "y", "c", "x"))
    key = ("z", "y", "c")
    in_specs = (P(key, None), P(key, "x", None), P(key, "x"))
    out_specs = (P(key), P(key, None))
    return jax.shard_map(local, mesh=fine, in_specs=in_specs, out_specs=out_specs, check_vma=False)
```

```python
import functools

import jax
import jax.numpy as jnp
from jax import lax
from jax.experimental import pallas as pl
from jax.experimental.pallas import tpu as pltpu
from jax.sharding import Mesh, PartitionSpec as P

D = 1024
SLAB = 1024
BR = 16
CAP = 2
NBLK = SLAB // BR
NBD = 64
KEYS = 64
NZ, NY, NC, NX = 8, 4, 2, 4
PEERS = NY * NC
PLANE = NX * PEERS
CX = D // NX
TEMP = 0.05
GROUPS = ((0, 1, 7), (2, 6), (3, 4, 5))

F32, BF16, I32 = jnp.float32, jnp.bfloat16, jnp.int32
NT = (((1,), (1,)), ((), ()))
TN = (((0,), (0,)), ((), ()))
SMEM = pl.BlockSpec(memory_space=pltpu.SMEM)


def pick_kernel(count, asked_ref, *refs):
    tables, out_ref = refs[:count], refs[count]
    for k, table_ref in enumerate(tables):

        def body(n, _, k=k, table_ref=table_ref):
            at = (n // CAP) * (count * CAP) + k * CAP + n % CAP
            out_ref[at] = table_ref[jnp.maximum(asked_ref[k, n], 0)]
            return 0

        lax.fori_loop(0, PLANE * CAP, body, 0)


def pick_blocks(asked, tables):
    count = len(tables)
    out = pl.pallas_call(
        functools.partial(pick_kernel, count),
        out_shape=jax.ShapeDtypeStruct((PLANE * count * CAP, BR, CX), BF16),
        in_specs=[SMEM] + [pl.BlockSpec(memory_space=pltpu.VMEM)] * count,
        out_specs=pl.BlockSpec(memory_space=pltpu.VMEM),
        compiler_params=pltpu.CompilerParams(vmem_limit_bytes=12 << 20),
        cost_estimate=pl.CostEstimate(flops=0, bytes_accessed=count << 20, transcendentals=0),
    )(asked, *[t.reshape(NBLK, BR, CX) for t in tables])
    return out.reshape(-1, CX)


def pair_kernel(group_ref, place_ref, emb_ref, *refs):
    count = len(GROUPS)
    inc_refs, (part_ref, rounded_ref, ownk_ref, credk_ref) = refs[:count], refs[count : count + 4]
    cred_refs, held_ref = refs[count + 4 : 2 * count + 4], refs[2 * count + 4]
    emb = emb_ref[...]
    slots = 16
    rows = slots * BR

    for g in range(count):
        cred_refs[g][...] = jnp.zeros_like(cred_refs[g])

    for first in range(0, NBD, slots):

        def fetch(j, _, first=first):
            at = pl.ds(pl.multiple_of((first + j) * BR, BR), BR)
            for g in range(count):

                @pl.when(group_ref[first + j] == g)
                def _(g=g):
                    for x in range(NX):
                        place = x * (inc_refs[g].shape[0] // NX) + place_ref[first + j]
                        part_ref[at, pl.ds(x * CX, CX)] = inc_refs[g][place]

            return 0

        lax.fori_loop(0, slots, fetch, 0)
        part = part_ref[pl.ds(first * BR, rows), :]
        cosine = lax.dot_general(emb, part, NT, preferred_element_type=F32)
        weight = jnp.exp((cosine - 1.0) * (1.0 / TEMP))
        rounded = weight.astype(BF16)
        rounded_ref[:, pl.ds(first * BR, rows)] = rounded
        lanes = weight[:, :128] + weight[:, 128:]
        if first == 0:
            ownk_ref[...] = lanes
        else:
            ownk_ref[...] += lanes
        credk_ref[:, pl.ds(first * BR, rows)] = jnp.sum(weight, axis=0, keepdims=True)
        held_ref[...] = lax.dot_general(rounded, emb, TN, preferred_element_type=F32).astype(BF16)

        def store(j, _, first=first):
            at = pl.ds(pl.multiple_of(j * BR, BR), BR)
            for g in range(count):

                @pl.when(group_ref[first + j] == g)
                def _(g=g):
                    for x in range(NX):
                        place = x * (cred_refs[g].shape[0] // NX) + place_ref[first + j]
                        cred_refs[g][place] = held_ref[at, pl.ds(x * CX, CX)]

            return 0

        lax.fori_loop(0, slots, store, 0)


def pair_weights(group, place, emb, incoming):
    shapes = [jax.ShapeDtypeStruct((PLANE * len(ks) * CAP, BR, CX), BF16) for ks in GROUPS]
    incoming = [a.reshape(s.shape) for a, s in zip(incoming, shapes)]
    out = pl.pallas_call(
        pair_kernel,
        out_shape=(
            pltpu.HBM((SLAB, D), BF16),
            pltpu.HBM((SLAB, SLAB), BF16),
            jax.ShapeDtypeStruct((SLAB, 128), F32),
            jax.ShapeDtypeStruct((1, SLAB), F32),
            *[pltpu.HBM(s.shape, s.dtype) for s in shapes],
        ),
        in_specs=[SMEM, SMEM] + [pl.BlockSpec()] * (1 + len(GROUPS)),
        scratch_shapes=[pltpu.VMEM((16 * BR, D), BF16)],
        compiler_params=pltpu.CompilerParams(vmem_limit_bytes=28 << 20),
        cost_estimate=pl.CostEstimate(
            flops=4 * SLAB * SLAB * D, bytes_accessed=14 << 20, transcendentals=SLAB * SLAB
        ),
    )(group, place, emb, *incoming)
    return out[:4], [a.reshape(-1, CX) for a in out[4:]]


def own_kernel(rounded_ref, part_ref, own_ref):
    own_ref[0] = jnp.dot(rounded_ref[...], part_ref[...], preferred_element_type=F32).astype(BF16)


def own_sums(rounded, part):
    return pl.pallas_call(
        own_kernel,
        grid=(NX,),
        out_shape=pltpu.HBM((NX, SLAB, CX), BF16),
        in_specs=[
            pl.BlockSpec((SLAB, SLAB), lambda x: (0, 0)),
            pl.BlockSpec((SLAB, CX), lambda x: (0, x)),
        ],
        out_specs=pl.BlockSpec((1, SLAB, CX), lambda x: (x, 0, 0)),
        compiler_params=pltpu.CompilerParams(vmem_limit_bytes=12 << 20),
        cost_estimate=pl.CostEstimate(
            flops=2 * SLAB * SLAB * D, bytes_accessed=6 << 20, transcendentals=0
        ),
    )(*[pltpu.with_memory_space_constraint(a, pltpu.HBM) for a in (rounded, part)])


def add_kernel(count, ks, firsts, asked_ref, back_ref, *refs):
    n_out = len(ks)
    recvs, outs, acc_ref = refs[: len(firsts)], refs[len(firsts) : -1], refs[-1]
    for i, k in enumerate(ks):
        acc_ref[...] = jnp.zeros_like(acc_ref)
        for n, (recv, (target, first)) in enumerate(zip(recvs, firsts)):
            if target == i:
                acc_ref[pl.ds(first, recv.shape[0])] += recv[...].astype(F32)

        def body(n, _, k=k):
            block = asked_ref[k, n]

            @pl.when(block >= 0)
            def _():
                at = (n // CAP) * (count * CAP) + k * CAP + n % CAP
                acc_ref[block] += back_ref[at].astype(F32)

            return 0

        lax.fori_loop(0, PLANE * CAP, body, 0)
        if n_out == 1 and len(outs) == 2:
            outs[0][...] = acc_ref[: NBLK // 2].astype(outs[0].dtype)
            outs[1][...] = acc_ref[NBLK // 2 :].astype(outs[1].dtype)
        else:
            outs[i][...] = acc_ref[...].astype(outs[i].dtype)


def add_credits(asked, back, count, ks, recvs, firsts, outs):
    vmem = pl.BlockSpec(memory_space=pltpu.VMEM)
    return pl.pallas_call(
        functools.partial(add_kernel, count, tuple(ks), tuple(firsts)),
        out_shape=tuple(jax.ShapeDtypeStruct((n, BR, CX), t) for n, t in outs),
        in_specs=[SMEM, vmem] + [vmem] * len(recvs),
        out_specs=(vmem,) * len(outs),
        scratch_shapes=[pltpu.VMEM((NBLK, BR, CX), F32)],
        compiler_params=pltpu.CompilerParams(vmem_limit_bytes=12 << 20),
        cost_estimate=pl.CostEstimate(
            flops=0, bytes_accessed=(2 + len(ks)) << 20, transcendentals=0
        ),
    )(asked, back.reshape(-1, BR, CX), *[r.reshape(-1, BR, CX) for r in recvs])


def shift(axis, by):
    n = lax.axis_size(axis)
    return [(i, (i + by) % n) for i in range(n)]


def up(a, axis):
    return lax.ppermute(a, axis, shift(axis, 1))


def down(a, axis):
    return lax.ppermute(a, axis, shift(axis, -1))


def in_plane(a):
    return lax.all_to_all(a, ("x", "y", "c"), 0, 0, tiled=True)


def gather_over_x(mine):
    me = lax.axis_index("x")
    half = SLAB // 2
    parts = [mine[:half], mine[half:]]
    ups = [up(p, "x") for p in parts]
    downs = [down(p, "x") for p in parts]
    far = [up(ups[0], "x"), down(downs[1], "x")]
    place = lambda out, a, row, k: lax.dynamic_update_slice(
        out, a, (row, lax.rem(me + k, NX) * CX)
    )
    out = jnp.concatenate([mine] * NX, axis=1)
    for p in range(2):
        out = place(out, ups[p], p * half, 3)
        out = place(out, downs[p], p * half, 1)
        out = place(out, far[p], p * half, 2)
    return out


def slot_rank(source_list):
    count = source_list.shape[0]
    same = source_list[:, None] == source_list[None, :]
    before = jnp.arange(count)[None, :] < jnp.arange(count)[:, None]
    return jnp.sum(jnp.logical_and(same, before), axis=1).astype(I32)


def local(embeddings, sources, blocks):
    me_x, me_z = lax.axis_index("x"), lax.axis_index("z")
    columns = lax.dynamic_slice_in_dim(embeddings, me_x * CX, CX, axis=1)
    half = SLAB // 2

    source, block = sources[0, :, 0], blocks[0]
    rank = slot_rank(source)
    far = lax.rem(source // PEERS - me_z + NZ, NZ)
    peer = source % PEERS
    cell = (peer * NZ + far) * CAP + rank
    cells = jnp.arange(KEYS * CAP, dtype=I32)
    wanted = jnp.sum(jnp.where(cell[:, None] == cells[None, :], block[:, None] + 1, 0), axis=0) - 1
    wanted = jnp.tile(wanted.reshape(PEERS, NZ * CAP), (NX, 1))
    asked = in_plane(jnp.pad(wanted, ((0, 0), (0, 128 - NZ * CAP))))[:, : NZ * CAP]
    asked = asked.reshape(PLANE, NZ, CAP).transpose(1, 0, 2).reshape(NZ, PLANE * CAP)

    tables = {0: columns}
    ups = downs = columns
    for step in range(1, NZ // 2):
        ups, downs = up(ups, "z"), down(downs, "z")
        tables[NZ - step], tables[step] = ups, downs
    tables[NZ // 2] = jnp.concatenate([up(ups[:half], "z"), down(downs[half:], "z")])
    asked_of = [jnp.stack([asked[k] for k in ks]) for ks in GROUPS]
    incoming = [
        in_plane(pick_blocks(a, [tables[k] for k in ks])) for a, ks in zip(asked_of, GROUPS)
    ]

    group, place = jnp.zeros_like(far), jnp.zeros_like(far)
    for g, ks in enumerate(GROUPS):
        for n, k in enumerate(ks):
            group = jnp.where(far == k, g, group)
            place = jnp.where(far == k, (peer * len(ks) + n) * CAP + rank, place)
    (part, rounded, own_k, credit_k), credits = pair_weights(group, place, embeddings, incoming)

    back = [None] * len(GROUPS)
    last = len(GROUPS) - 1
    back[last] = in_plane(credits[last])
    own = own_sums(rounded, part)
    own_w = lax.psum_scatter(own, "x", tiled=True)[0]

    per_slot = credit_k.astype(BF16).reshape(NBD, BR)
    every = jnp.arange(KEYS * NBLK, dtype=I32)
    spread_k = ((source * NBLK + block)[:, None] == every[None, :]).astype(BF16)
    dense_k = lax.dot_general(per_slot, spread_k, TN, preferred_element_type=F32)

    assert all(k in ks and NZ - k in ks for k, ks in zip((1, 2, 3), GROUPS))
    where = {k: (g, n) for g, ks in enumerate(GROUPS) for n, k in enumerate(ks)}

    def add(ks, recvs, firsts, outs):
        g = where[ks[0]][0]
        return add_credits(
            asked_of[g], back[g], len(GROUPS[g]), [where[k][1] for k in ks], recvs, firsts, outs
        )

    to_up, to_down = add([NZ // 2], [], [], [(NBLK // 2, BF16)] * 2)
    for k in range(NZ // 2 - 1, 0, -1):
        if k > 1:
            to_up, to_down, credit = lax.optimization_barrier((to_up, to_down, credits[k - 2]))
            back[k - 2] = in_plane(credit)
        from_down, from_up = up(to_up, "z"), down(to_down, "z")
        firsts = [(0, 0), (1, NBLK // 2 if k == NZ // 2 - 1 else 0)]
        to_up, to_down = add([k, NZ - k], [from_down, from_up], firsts, [(NBLK, BF16)] * 2)
        if k == 2:
            to_up, to_down, dense_k = lax.optimization_barrier((to_up, to_down, dense_k))
    from_down, from_up = up(to_up, "z"), down(to_down, "z")
    (got,) = add([0], [from_down, from_up], [(0, 0), (0, 0)], [(NBLK, F32)])

    all_k = lax.all_to_all(dense_k.reshape(BR, KEYS, NBLK), ("z", "y", "c"), 1, 0, tiled=True)
    got_k = jnp.sum(all_k.reshape(KEYS, BR, NBLK), axis=0).T.reshape(SLAB)
    scale = 1.0 + lax.psum(got_k + jnp.sum(own_k, axis=1), "x")

    got, own_w, scale = lax.optimization_barrier((got, own_w, scale))
    total_w = own_w.astype(F32) + got.reshape(SLAB, CX)
    mean = ((columns.astype(F32) + total_w) / scale[:, None]).astype(BF16)
    return jnp.log(scale), gather_over_x(lax.optimization_barrier(mean))


def solution(mesh):
    fine = Mesh(mesh.devices.reshape(NZ, NY, NC, NX), ("z", "y", "c", "x"))
    key = ("z", "y", "c")
    in_specs = (P(key, None), P(key, "x", None), P(key, "x"))
    out_specs = (P(key), P(key, None))
    return jax.shard_map(local, mesh=fine, in_specs=in_specs, out_specs=out_specs, check_vma=False)
```

```python
import jax
import jax.numpy as jnp
from jax import lax
from jax.experimental import pallas as pl
from jax.experimental.pallas import tpu as pltpu
from jax.sharding import Mesh, PartitionSpec as P

D = 1024
SLAB = 1024
BR = 16
NBLK = SLAB // BR
NBD = 64
KEYS = 64
NZ, NY, NC, NX = 8, 4, 2, 4
PIECES = NY * NC
RP = BR // PIECES
CX = D // NX
W = RP * CX
PLANE = NX * NY * NC
TEMP = 0.05

F32, BF16 = jnp.float32, jnp.bfloat16
NT = (((1,), (1,)), ((), ()))
TN = (((0,), (0,)), ((), ()))


def pair_kernel(emb_ref, inc_ref, part_ref, rounded_ref, ownk_ref, cred_ref, credk_ref):
    emb = emb_ref[...]
    group = NC * RP * NBD
    for y in range(NY):
        for c in range(NC):
            for r in range(RP):
                for x in range(NX):
                    part_ref[pl.ds(y * group + (c * RP + r) * NBD, NBD), pl.ds(x * CX, CX)] = inc_ref[
                        x, NC * y + c, :, pl.ds(r * CX, CX)
                    ]
        part = part_ref[pl.ds(y * group, group), :]
        cosine = lax.dot_general(emb, part, NT, preferred_element_type=F32)
        weight = jnp.exp((cosine - 1.0) * (1.0 / TEMP))
        rounded = weight.astype(BF16)
        rounded_ref[:, pl.ds(y * group, group)] = rounded
        lanes = weight[:, :128] + weight[:, 128:]
        if y == 0:
            ownk_ref[...] = lanes
        else:
            ownk_ref[...] += lanes
        credk_ref[:, pl.ds(y * group, group)] = jnp.sum(weight, axis=0, keepdims=True)
        cred = lax.dot_general(rounded, emb, TN, preferred_element_type=F32).astype(BF16)
        for c in range(NC):
            for r in range(RP):
                at = (c * RP + r) * NBD
                for x in range(NX):
                    cred_ref[x, NC * y + c, :, pl.ds(r * CX, CX)] = cred[
                        at : at + NBD, x * CX : (x + 1) * CX
                    ]


def pair_weights(emb, inc):
    return pl.pallas_call(
        pair_kernel,
        out_shape=(
            pltpu.HBM((SLAB, D), BF16),
            pltpu.HBM((SLAB, SLAB), BF16),
            jax.ShapeDtypeStruct((SLAB, 128), F32),
            pltpu.HBM((NX, PIECES, NBD, W), BF16),
            jax.ShapeDtypeStruct((1, SLAB), F32),
        ),
        compiler_params=pltpu.CompilerParams(vmem_limit_bytes=20 << 20),
        cost_estimate=pl.CostEstimate(
            flops=4 * SLAB * SLAB * D, bytes_accessed=10 << 20, transcendentals=SLAB * SLAB
        ),
    )(emb, inc.reshape(NX, PIECES, NBD, W))


def own_kernel(rounded_ref, part_ref, own_ref):
    own_ref[0] = jnp.dot(rounded_ref[...], part_ref[...], preferred_element_type=F32).astype(BF16)


def own_sums(rounded, part):
    return pl.pallas_call(
        own_kernel,
        grid=(NX,),
        out_shape=pltpu.HBM((NX, SLAB, CX), BF16),
        in_specs=[
            pl.BlockSpec((SLAB, SLAB), lambda x: (0, 0)),
            pl.BlockSpec((SLAB, CX), lambda x: (0, x)),
        ],
        out_specs=pl.BlockSpec((1, SLAB, CX), lambda x: (x, 0, 0)),
        compiler_params=pltpu.CompilerParams(vmem_limit_bytes=12 << 20),
        cost_estimate=pl.CostEstimate(
            flops=2 * SLAB * SLAB * D, bytes_accessed=6 << 20, transcendentals=0
        ),
    )(*[pltpu.with_memory_space_constraint(a, pltpu.HBM) for a in (rounded, part)])


def shift(axis, by):
    n = lax.axis_size(axis)
    return [(i, (i + by) % n) for i in range(n)]


def up(a, axis):
    return lax.ppermute(a, axis, shift(axis, 1))


def down(a, axis):
    return lax.ppermute(a, axis, shift(axis, -1))


def gather_over_x(mine):
    me = lax.axis_index("x")
    half = SLAB // 2
    parts = [mine[:half], mine[half:]]
    ups = [up(p, "x") for p in parts]
    downs = [down(p, "x") for p in parts]
    far = [up(ups[0], "x"), down(downs[1], "x")]
    place = lambda out, a, row, k: lax.dynamic_update_slice(
        out, a, (row, lax.rem(me + k, NX) * CX)
    )
    out = jnp.concatenate([mine] * NX, axis=1)
    for p in range(2):
        out = place(out, ups[p], p * half, 3)
        out = place(out, downs[p], p * half, 1)
        out = place(out, far[p], p * half, 2)
    return out


def share_in_plane(wanted):
    padded = jnp.broadcast_to(jnp.pad(wanted, (0, 128 - NBD)), (PLANE, 128))
    return lax.all_to_all(padded, ("x", "y", "c"), 0, 0, tiled=True)[:, :NBD].reshape(-1)


def pick_over_z(held, plane_wanted):
    me = lax.axis_index("z")
    rows = held.shape[0]
    half = rows // 2
    inside = jnp.arange(rows, dtype=jnp.int32)
    picked = None

    def take(picked, parts):
        at = jnp.concatenate(
            [lax.rem(me + k, NZ) * rows + inside[first : first + t.shape[0]] for k, first, t in parts]
        )
        pick = (plane_wanted[:, None] == at[None, :]).astype(BF16)
        got = jnp.dot(pick, jnp.concatenate([t for _, _, t in parts]), preferred_element_type=F32)
        return (got if picked is None else got + picked.astype(F32)).astype(BF16)

    ups = downs = [held[:half], held[half:]]
    picked = take(None, [(0, 0, held)])
    for step in range(1, NZ // 2):
        ups = [up(t, "z") for t in ups]
        downs = [down(t, "z") for t in downs]
        picked = take(
            picked,
            [(NZ - step, p * half, ups[p]) for p in range(2)]
            + [(step, p * half, downs[p]) for p in range(2)],
        )
    far = [(NZ // 2, 0, up(ups[0], "z")), (NZ // 2, half, down(downs[1], "z"))]
    return take(picked, far)


def sum_over_z(back, plane_wanted, later):
    me = lax.axis_index("z")
    rows = PIECES * NBLK
    half = rows // 2
    inside = jnp.arange(rows, dtype=jnp.int32)

    def table(k, first, last):
        at = lax.rem(me + k, NZ) * rows + inside[first:last]
        spread = (at[:, None] == plane_wanted[None, :]).astype(BF16)
        return jnp.dot(spread, back, preferred_element_type=F32)

    far = NZ // 2
    ups = up(table(far, 0, half).astype(BF16), "z")
    downs = down(table(far, half, rows).astype(BF16), "z")
    for k in range(far - 1, 0, -1):
        if k == far - 2:
            ups, downs, later = lax.optimization_barrier((ups, downs, later))
        if k == far - 1:
            add_up = jnp.concatenate([ups.astype(F32), jnp.zeros((half, W), F32)])
            add_down = jnp.concatenate([jnp.zeros((half, W), F32), downs.astype(F32)])
        else:
            add_up, add_down = ups.astype(F32), downs.astype(F32)
        ups = up((table(k, 0, rows) + add_up).astype(BF16), "z")
        downs = down((table(NZ - k, 0, rows) + add_down).astype(BF16), "z")
    return (table(0, 0, rows) + (ups.astype(F32) + downs.astype(F32))).astype(BF16), later


def local(embeddings, sources, blocks):
    me_x = lax.axis_index("x")
    me_key = lax.axis_index(("z", "y", "c"))
    columns = lax.dynamic_slice_in_dim(embeddings, me_x * CX, CX, axis=1)
    pieces = columns.reshape(NBLK, PIECES, W).transpose(1, 0, 2).reshape(PIECES * NBLK, W)
    held = lax.all_to_all(pieces, ("y", "c"), 0, 0, tiled=True)

    wanted = sources[0, :, 0] * NBLK + blocks[0]
    held, late = lax.optimization_barrier((held, wanted))
    plane_wanted = share_in_plane(late)
    outgoing = pick_over_z(held, plane_wanted)
    incoming = lax.all_to_all(outgoing, ("x", "y", "c"), 0, 0, tiled=True)

    part, rounded, own_k, credit, credit_k = pair_weights(embeddings, incoming)
    credit = credit.reshape(PLANE * NBD, W)
    back = lax.all_to_all(credit, ("x", "y", "c"), 0, 0, tiled=True)
    back, own = lax.optimization_barrier((back, own_sums(rounded, part)))
    own_w = lax.psum_scatter(own, "x", tiled=True)[0]

    per_slot = credit_k.astype(BF16).reshape(BR, NBD)
    every = jnp.arange(KEYS * NBLK, dtype=jnp.int32)
    spread_k = (wanted[:, None] == every[None, :]).astype(BF16)
    dense_k = jnp.dot(per_slot, spread_k, preferred_element_type=F32)
    dense_k = dense_k.reshape(BR, NZ, PIECES * NBLK).transpose(1, 0, 2)
    plane_k = lax.psum_scatter(dense_k, "z", tiled=True)[0]

    got, plane_k = sum_over_z(back, plane_wanted, plane_k)
    all_k = lax.all_to_all(plane_k.reshape(BR, PIECES, NBLK), ("y", "c"), 1, 0, tiled=True)
    got_k = jnp.sum(all_k.reshape(PIECES, BR, NBLK), axis=0).T.reshape(SLAB) + jnp.sum(own_k, axis=1)
    got, own_w, got_k = lax.optimization_barrier((got, own_w, got_k))
    scale = 1.0 + lax.psum(got_k, "x")
    got = lax.all_to_all(got, ("y", "c"), 0, 0, tiled=True)
    rows = jnp.arange(SLAB, dtype=jnp.int32)
    source = (rows % RP) * (SLAB // RP) + (rows % BR) // RP * NBLK + rows // BR
    got = got.reshape(PIECES * NBLK, W)
    got = jnp.concatenate([got[:, r * CX : (r + 1) * CX] for r in range(RP)])
    order = (source[:, None] == rows[None, :]).astype(BF16)
    total_w = own_w.astype(F32) + jnp.dot(order, got, preferred_element_type=F32)
    mean = ((columns.astype(F32) + total_w) / scale[:, None]).astype(BF16)
    return jnp.log(scale), gather_over_x(lax.optimization_barrier(mean))


def solution(mesh):
    fine = Mesh(mesh.devices.reshape(NZ, NY, NC, NX), ("z", "y", "c", "x"))
    key = ("z", "y", "c")
    in_specs = (P(key, None), P(key, "x", None), P(key, "x"))
    out_specs = (P(key), P(key, None))
    return jax.shard_map(local, mesh=fine, in_specs=in_specs, out_specs=out_specs, check_vma=False)
```

```python
import jax
import jax.numpy as jnp
from jax import lax
from jax.experimental import pallas as pl
from jax.experimental.pallas import tpu as pltpu
from jax.sharding import Mesh, PartitionSpec as P

D = 1024
SLAB = 1024
BR = 16
NBLK = SLAB // BR
NBD = 64
KEYS = 64
NZ, NY, NC, NX = 8, 4, 2, 4
PIECES = NY * NC
RP = BR // PIECES
CX = D // NX
W = RP * CX
PLANE = NX * NY * NC
TEMP = 0.05

F32, BF16 = jnp.float32, jnp.bfloat16
NT = (((1,), (1,)), ((), ()))
TN = (((0,), (0,)), ((), ()))


def pair_kernel(emb_ref, inc_ref, part_ref, rounded_ref, ownk_ref, cred_ref, credk_ref):
    emb = emb_ref[...]
    group = NC * RP * NBD
    for y in range(NY):
        for c in range(NC):
            for r in range(RP):
                for x in range(NX):
                    part_ref[pl.ds(y * group + (c * RP + r) * NBD, NBD), pl.ds(x * CX, CX)] = inc_ref[
                        x, NC * y + c, :, pl.ds(r * CX, CX)
                    ]
        part = part_ref[pl.ds(y * group, group), :]
        cosine = lax.dot_general(emb, part, NT, preferred_element_type=F32)
        weight = jnp.exp((cosine - 1.0) * (1.0 / TEMP))
        rounded = weight.astype(BF16)
        rounded_ref[:, pl.ds(y * group, group)] = rounded
        lanes = weight[:, :128] + weight[:, 128:]
        if y == 0:
            ownk_ref[...] = lanes
        else:
            ownk_ref[...] += lanes
        credk_ref[:, pl.ds(y * group, group)] = jnp.sum(weight, axis=0, keepdims=True)
        cred = lax.dot_general(rounded, emb, TN, preferred_element_type=F32).astype(BF16)
        for c in range(NC):
            for r in range(RP):
                at = (c * RP + r) * NBD
                for x in range(NX):
                    cred_ref[x, NC * y + c, :, pl.ds(r * CX, CX)] = cred[
                        at : at + NBD, x * CX : (x + 1) * CX
                    ]


def pair_weights(emb, inc):
    return pl.pallas_call(
        pair_kernel,
        out_shape=(
            pltpu.HBM((SLAB, D), BF16),
            pltpu.HBM((SLAB, SLAB), BF16),
            jax.ShapeDtypeStruct((SLAB, 128), F32),
            pltpu.HBM((NX, PIECES, NBD, W), BF16),
            jax.ShapeDtypeStruct((1, SLAB), F32),
        ),
        compiler_params=pltpu.CompilerParams(vmem_limit_bytes=20 << 20),
        cost_estimate=pl.CostEstimate(
            flops=4 * SLAB * SLAB * D, bytes_accessed=10 << 20, transcendentals=SLAB * SLAB
        ),
    )(emb, inc.reshape(NX, PIECES, NBD, W))


def own_kernel(rounded_ref, part_ref, own_ref):
    own_ref[0] = jnp.dot(rounded_ref[...], part_ref[...], preferred_element_type=F32).astype(BF16)


def own_sums(rounded, part):
    return pl.pallas_call(
        own_kernel,
        grid=(NX,),
        out_shape=pltpu.HBM((NX, SLAB, CX), BF16),
        in_specs=[
            pl.BlockSpec((SLAB, SLAB), lambda x: (0, 0)),
            pl.BlockSpec((SLAB, CX), lambda x: (0, x)),
        ],
        out_specs=pl.BlockSpec((1, SLAB, CX), lambda x: (x, 0, 0)),
        compiler_params=pltpu.CompilerParams(vmem_limit_bytes=12 << 20),
        cost_estimate=pl.CostEstimate(
            flops=2 * SLAB * SLAB * D, bytes_accessed=6 << 20, transcendentals=0
        ),
    )(*[pltpu.with_memory_space_constraint(a, pltpu.HBM) for a in (rounded, part)])


def shift(axis, by):
    n = lax.axis_size(axis)
    return [(i, (i + by) % n) for i in range(n)]


def up(a, axis):
    return lax.ppermute(a, axis, shift(axis, 1))


def down(a, axis):
    return lax.ppermute(a, axis, shift(axis, -1))


def gather_over_x(mine):
    me = lax.axis_index("x")
    half = SLAB // 2
    parts = [mine[:half], mine[half:]]
    ups = [up(p, "x") for p in parts]
    downs = [down(p, "x") for p in parts]
    far = [up(ups[0], "x"), down(downs[1], "x")]
    place = lambda out, a, row, k: lax.dynamic_update_slice(
        out, a, (row, lax.rem(me + k, NX) * CX)
    )
    out = jnp.concatenate([mine] * NX, axis=1)
    for p in range(2):
        out = place(out, ups[p], p * half, 3)
        out = place(out, downs[p], p * half, 1)
        out = place(out, far[p], p * half, 2)
    return out


def share_in_plane(wanted):
    padded = jnp.broadcast_to(jnp.pad(wanted, (0, 128 - NBD)), (PLANE, 128))
    return lax.all_to_all(padded, ("x", "y", "c"), 0, 0, tiled=True)[:, :NBD].reshape(-1)


def pick_over_z(held, plane_wanted):
    me = lax.axis_index("z")
    rows = held.shape[0]
    half = rows // 2
    inside = jnp.arange(rows, dtype=jnp.int32)
    picked = None

    def take(picked, parts):
        at = jnp.concatenate(
            [lax.rem(me + k, NZ) * rows + inside[first : first + t.shape[0]] for k, first, t in parts]
        )
        pick = (plane_wanted[:, None] == at[None, :]).astype(BF16)
        got = jnp.dot(pick, jnp.concatenate([t for _, _, t in parts]), preferred_element_type=F32)
        return (got if picked is None else got + picked.astype(F32)).astype(BF16)

    ups = downs = [held[:half], held[half:]]
    picked = take(None, [(0, 0, held)])
    for step in range(1, NZ // 2):
        ups = [up(t, "z") for t in ups]
        downs = [down(t, "z") for t in downs]
        picked = take(
            picked,
            [(NZ - step, p * half, ups[p]) for p in range(2)]
            + [(step, p * half, downs[p]) for p in range(2)],
        )
    far = [(NZ // 2, 0, up(ups[0], "z")), (NZ // 2, half, down(downs[1], "z"))]
    return take(picked, far)


def credit_kernel(at_ref, wanted_ref, back_ref, *refs):
    n_out = at_ref.shape[0]
    arrived, outs = refs[:-n_out], refs[-n_out:]
    each = len(arrived) // n_out
    rows = outs[0].shape[0]
    for i, out_ref in enumerate(outs):
        row = at_ref[i] + lax.broadcasted_iota(jnp.int32, (rows, PLANE * NBD), 0)
        spread = jnp.where(row == wanted_ref[...], 1.0, 0.0).astype(BF16)
        total = jnp.dot(spread, back_ref[...], preferred_element_type=F32)
        for a in arrived[i * each : (i + 1) * each]:
            total += a[...].astype(F32)
        out_ref[...] = total.astype(BF16)


def credit_sums(at, wanted, back, arrived):
    rows = PIECES * NBLK // 2
    vmem = pl.BlockSpec(memory_space=pltpu.VMEM)
    n_out = len(at)
    return pl.pallas_call(
        credit_kernel,
        out_shape=(jax.ShapeDtypeStruct((rows, W), BF16),) * n_out,
        in_specs=[pl.BlockSpec(memory_space=pltpu.SMEM)] + [vmem] * (2 + len(arrived)),
        out_specs=(vmem,) * n_out,
        compiler_params=pltpu.CompilerParams(vmem_limit_bytes=12 << 20),
        cost_estimate=pl.CostEstimate(
            flops=2 * n_out * rows * PLANE * NBD * W, bytes_accessed=3 << 20, transcendentals=0
        ),
    )(jnp.stack(at), wanted, back, *arrived)


def sum_over_z(back, plane_wanted, later):
    me = lax.axis_index("z")
    rows = PIECES * NBLK
    wanted = plane_wanted[None, :]

    def sums(targets, arrived=()):
        at = [lax.rem(me + k, NZ) * rows + part * (rows // 2) for k, part in targets]
        return credit_sums(at, wanted, back, arrived)

    far = NZ // 2
    first = sums([(far, 0), (far, 1)])
    ups, downs = [up(first[0], "z"), None], [None, down(first[1], "z")]
    second = sums([(far - 1, 1), (far + 1, 0)])
    ups[1], downs[0] = up(second[0], "z"), down(second[1], "z")
    third = sums([(far - 1, 0), (far + 1, 1)], [ups[0], downs[1]])
    ups[0], downs[1] = up(third[0], "z"), down(third[1], "z")
    ups[1], later = lax.optimization_barrier((ups[1], later))
    for k in range(far - 2, 0, -1):
        for p in range(2):
            sent = sums([(k, 1 - p), (NZ - k, p)], [ups[1 - p], downs[p]])
            ups[1 - p], downs[p] = up(sent[0], "z"), down(sent[1], "z")
    last = [sums([(0, p)], [ups[p], downs[p]])[0] for p in range(2)]
    return jnp.concatenate(last), later


def local(embeddings, sources, blocks):
    me_x = lax.axis_index("x")
    me_key = lax.axis_index(("z", "y", "c"))
    columns = lax.dynamic_slice_in_dim(embeddings, me_x * CX, CX, axis=1)
    pieces = columns.reshape(NBLK, PIECES, W).transpose(1, 0, 2).reshape(PIECES * NBLK, W)
    held = lax.all_to_all(pieces, ("y", "c"), 0, 0, tiled=True)

    wanted = sources[0, :, 0] * NBLK + blocks[0]
    held, late = lax.optimization_barrier((held, wanted))
    plane_wanted = share_in_plane(late)
    outgoing = pick_over_z(held, plane_wanted)
    incoming = lax.all_to_all(outgoing, ("x", "y", "c"), 0, 0, tiled=True)

    part, rounded, own_k, credit, credit_k = pair_weights(embeddings, incoming)
    credit = credit.reshape(PLANE * NBD, W)
    back = lax.all_to_all(credit, ("x", "y", "c"), 0, 0, tiled=True)
    back, own = lax.optimization_barrier((back, own_sums(rounded, part)))
    own_w = lax.psum_scatter(own, "x", tiled=True)[0]

    per_slot = credit_k.astype(BF16).reshape(BR, NBD)
    every = jnp.arange(KEYS * NBLK, dtype=jnp.int32)
    spread_k = (wanted[:, None] == every[None, :]).astype(BF16)
    dense_k = jnp.dot(per_slot, spread_k, preferred_element_type=F32)
    dense_k = dense_k.reshape(BR, NZ, PIECES * NBLK).transpose(1, 0, 2)
    plane_k = lax.psum_scatter(dense_k, "z", tiled=True)[0]

    got, plane_k = sum_over_z(back, plane_wanted, plane_k)
    all_k = lax.all_to_all(plane_k.reshape(BR, PIECES, NBLK), ("y", "c"), 1, 0, tiled=True)
    got_k = jnp.sum(all_k.reshape(PIECES, BR, NBLK), axis=0).T.reshape(SLAB) + jnp.sum(own_k, axis=1)
    got, own_w, got_k = lax.optimization_barrier((got, own_w, got_k))
    scale = 1.0 + lax.psum(got_k, "x")
    got = lax.all_to_all(got, ("y", "c"), 0, 0, tiled=True)
    rows = jnp.arange(SLAB, dtype=jnp.int32)
    source = (rows % RP) * (SLAB // RP) + (rows % BR) // RP * NBLK + rows // BR
    got = got.reshape(PIECES * NBLK, W)
    got = jnp.concatenate([got[:, r * CX : (r + 1) * CX] for r in range(RP)])
    order = (source[:, None] == rows[None, :]).astype(BF16)
    total_w = own_w.astype(F32) + jnp.dot(order, got, preferred_element_type=F32)
    mean = ((columns.astype(F32) + total_w) / scale[:, None]).astype(BF16)
    return jnp.log(scale), gather_over_x(lax.optimization_barrier(mean))


def solution(mesh):
    fine = Mesh(mesh.devices.reshape(NZ, NY, NC, NX), ("z", "y", "c", "x"))
    key = ("z", "y", "c")
    in_specs = (P(key, None), P(key, "x", None), P(key, "x"))
    out_specs = (P(key), P(key, None))
    return jax.shard_map(local, mesh=fine, in_specs=in_specs, out_specs=out_specs, check_vma=False)
```

```python
import jax
import jax.numpy as jnp
from jax import lax
from jax.experimental import pallas as pl
from jax.experimental.pallas import tpu as pltpu
from jax.sharding import Mesh, PartitionSpec as P

D = 1024
SLAB = 1024
BR = 16
NBLK = SLAB // BR
NBD = 64
KEYS = 64
NZ, NY, NC, NX = 8, 4, 2, 4
PIECES = NY * NC
RP = BR // PIECES
CX = D // NX
W = RP * CX
PLANE = NX * NY * NC
TEMP = 0.05

F32, BF16 = jnp.float32, jnp.bfloat16
NT = (((1,), (1,)), ((), ()))
TN = (((0,), (0,)), ((), ()))


def pair_kernel(emb_ref, inc_ref, part_ref, rounded_ref, ownk_ref, cred_ref, credk_ref):
    emb = emb_ref[...]
    group = NC * RP * NBD
    for y in range(NY):
        for c in range(NC):
            for r in range(RP):
                for x in range(NX):
                    part_ref[pl.ds(y * group + (c * RP + r) * NBD, NBD), pl.ds(x * CX, CX)] = inc_ref[
                        x, NC * y + c, :, pl.ds(r * CX, CX)
                    ]
        part = part_ref[pl.ds(y * group, group), :]
        cosine = lax.dot_general(part, emb, NT, preferred_element_type=F32)
        weight = jnp.exp((cosine - 1.0) * (1.0 / TEMP))
        rounded = weight.astype(BF16)
        rounded_ref[pl.ds(y * group, group), :] = rounded
        ownk = jnp.sum(weight, axis=0, keepdims=True)
        if y == 0:
            ownk_ref[...] = ownk
        else:
            ownk_ref[...] += ownk
        credk_ref[pl.ds(y * group, group), :] = sum(weight[:, n : n + 128] for n in range(0, SLAB, 128))
        cred = jnp.dot(rounded, emb, preferred_element_type=F32).astype(BF16)
        for c in range(NC):
            for r in range(RP):
                at = (c * RP + r) * NBD
                for x in range(NX):
                    cred_ref[x, NC * y + c, :, pl.ds(r * CX, CX)] = cred[
                        at : at + NBD, x * CX : (x + 1) * CX
                    ]


def pair_weights(emb, inc):
    return pl.pallas_call(
        pair_kernel,
        out_shape=(
            pltpu.HBM((SLAB, D), BF16),
            pltpu.HBM((SLAB, SLAB), BF16),
            jax.ShapeDtypeStruct((1, SLAB), F32),
            pltpu.HBM((NX, PIECES, NBD, W), BF16),
            jax.ShapeDtypeStruct((SLAB, 128), F32),
        ),
        compiler_params=pltpu.CompilerParams(vmem_limit_bytes=20 << 20),
        cost_estimate=pl.CostEstimate(
            flops=4 * SLAB * SLAB * D, bytes_accessed=10 << 20, transcendentals=SLAB * SLAB
        ),
    )(emb, inc.reshape(NX, PIECES, NBD, W))


def own_kernel(rounded_ref, part_ref, own_ref):
    own = lax.dot_general(rounded_ref[...], part_ref[...], TN, preferred_element_type=F32)
    own_ref[0] = own.astype(BF16)


def own_sums(rounded, part):
    return pl.pallas_call(
        own_kernel,
        grid=(NX,),
        out_shape=pltpu.HBM((NX, SLAB, CX), BF16),
        in_specs=[
            pl.BlockSpec((SLAB, SLAB), lambda x: (0, 0)),
            pl.BlockSpec((SLAB, CX), lambda x: (0, x)),
        ],
        out_specs=pl.BlockSpec((1, SLAB, CX), lambda x: (x, 0, 0)),
        compiler_params=pltpu.CompilerParams(vmem_limit_bytes=12 << 20),
        cost_estimate=pl.CostEstimate(
            flops=2 * SLAB * SLAB * D, bytes_accessed=6 << 20, transcendentals=0
        ),
    )(*[pltpu.with_memory_space_constraint(a, pltpu.HBM) for a in (rounded, part)])


def shift(axis, by):
    n = lax.axis_size(axis)
    return [(i, (i + by) % n) for i in range(n)]


def up(a, axis):
    return lax.ppermute(a, axis, shift(axis, 1))


def down(a, axis):
    return lax.ppermute(a, axis, shift(axis, -1))


def gather_over_x(mine):
    me = lax.axis_index("x")
    half = SLAB // 2
    parts = [mine[:half], mine[half:]]
    ups = [up(p, "x") for p in parts]
    downs = [down(p, "x") for p in parts]
    far = [up(ups[0], "x"), down(downs[1], "x")]
    place = lambda out, a, row, k: lax.dynamic_update_slice(
        out, a, (row, lax.rem(me + k, NX) * CX)
    )
    out = jnp.concatenate([mine] * NX, axis=1)
    for p in range(2):
        out = place(out, ups[p], p * half, 3)
        out = place(out, downs[p], p * half, 1)
        out = place(out, far[p], p * half, 2)
    return out


def share_in_plane(wanted):
    padded = jnp.broadcast_to(jnp.pad(wanted, (0, 128 - NBD)), (PLANE, 128))
    return lax.all_to_all(padded, ("x", "y", "c"), 0, 0, tiled=True)[:, :NBD].reshape(-1)


def pick_over_z(held, plane_wanted):
    me = lax.axis_index("z")
    rows = held.shape[0]
    half = rows // 2
    inside = jnp.arange(rows, dtype=jnp.int32)
    picked = None

    def take(picked, parts):
        at = jnp.concatenate(
            [lax.rem(me + k, NZ) * rows + inside[first : first + t.shape[0]] for k, first, t in parts]
        )
        pick = (plane_wanted[:, None] == at[None, :]).astype(BF16)
        got = jnp.dot(pick, jnp.concatenate([t for _, _, t in parts]), preferred_element_type=F32)
        return (got if picked is None else got + picked.astype(F32)).astype(BF16)

    ups = downs = [held[:half], held[half:]]
    picked = take(None, [(0, 0, held)])
    for step in range(1, NZ // 2):
        ups = [up(t, "z") for t in ups]
        downs = [down(t, "z") for t in downs]
        picked = take(
            picked,
            [(NZ - step, p * half, ups[p]) for p in range(2)]
            + [(step, p * half, downs[p]) for p in range(2)],
        )
    far = [(NZ // 2, 0, up(ups[0], "z")), (NZ // 2, half, down(downs[1], "z"))]
    return take(picked, far)


def credit_kernel(at_ref, wanted_ref, back_ref, *refs):
    n_out = at_ref.shape[0]
    arrived, outs = refs[:-n_out], refs[-n_out:]
    each = len(arrived) // n_out
    rows = outs[0].shape[0]
    iota = lax.broadcasted_iota(jnp.int32, (rows, PLANE * NBD), 0)
    spread = jnp.concatenate(
        [jnp.where(at_ref[i] + iota == wanted_ref[...], 1.0, 0.0).astype(BF16) for i in range(n_out)]
    )
    total = jnp.dot(spread, back_ref[...], preferred_element_type=F32)
    for i, out_ref in enumerate(outs):
        sums = total[i * rows : (i + 1) * rows]
        for a in arrived[i * each : (i + 1) * each]:
            sums += a[...].astype(F32)
        out_ref[...] = sums.astype(BF16)


def credit_sums(at, wanted, back, arrived):
    rows = PIECES * NBLK // 2
    vmem = pl.BlockSpec(memory_space=pltpu.VMEM)
    n_out = len(at)
    return pl.pallas_call(
        credit_kernel,
        out_shape=(jax.ShapeDtypeStruct((rows, W), BF16),) * n_out,
        in_specs=[pl.BlockSpec(memory_space=pltpu.SMEM)] + [vmem] * (2 + len(arrived)),
        out_specs=(vmem,) * n_out,
        compiler_params=pltpu.CompilerParams(vmem_limit_bytes=12 << 20),
        cost_estimate=pl.CostEstimate(
            flops=2 * n_out * rows * PLANE * NBD * W, bytes_accessed=3 << 20, transcendentals=0
        ),
    )(jnp.stack(at), wanted, back, *arrived)


def exchange_k(plane_k):
    all_k = lax.all_to_all(plane_k.reshape(BR, PIECES, NBLK), ("y", "c"), 1, 0, tiled=True)
    return jnp.sum(all_k.reshape(PIECES, BR, NBLK), axis=0).T.reshape(SLAB)


def sum_over_z(back, plane_wanted, later):
    me = lax.axis_index("z")
    rows = PIECES * NBLK
    wanted = plane_wanted[None, :]

    def sums(targets, arrived=()):
        at = [lax.rem(me + k, NZ) * rows + part * (rows // 2) for k, part in targets]
        return credit_sums(at, wanted, back, arrived)

    far = NZ // 2
    first = sums([(far, 0), (far, 1)])
    ups, downs = [up(first[0], "z"), None], [None, down(first[1], "z")]
    second = sums([(far - 1, 1), (far + 1, 0)])
    ups[1], downs[0] = up(second[0], "z"), down(second[1], "z")
    third = sums([(far - 1, 0), (far + 1, 1)], [ups[0], downs[1]])
    ups[0], downs[1] = up(third[0], "z"), down(third[1], "z")
    ups[1], later = lax.optimization_barrier((ups[1], later))
    later = exchange_k(later)
    for k in range(far - 2, 0, -1):
        for p in range(2):
            if k == 1 and p == 0:
                ups[1], later = lax.optimization_barrier((ups[1], later))
            sent = sums([(k, 1 - p), (NZ - k, p)], [ups[1 - p], downs[p]])
            ups[1 - p], downs[p] = up(sent[0], "z"), down(sent[1], "z")
    last = [sums([(0, p)], [ups[p], downs[p]])[0] for p in range(2)]
    return jnp.concatenate(last), later


def local(embeddings, sources, blocks):
    me_x = lax.axis_index("x")
    me_key = lax.axis_index(("z", "y", "c"))
    columns = lax.dynamic_slice_in_dim(embeddings, me_x * CX, CX, axis=1)
    pieces = columns.reshape(NBLK, PIECES, W).transpose(1, 0, 2).reshape(PIECES * NBLK, W)
    held = lax.all_to_all(pieces, ("y", "c"), 0, 0, tiled=True)

    wanted = sources[0, :, 0] * NBLK + blocks[0]
    held, late = lax.optimization_barrier((held, wanted))
    plane_wanted = share_in_plane(late)
    outgoing = pick_over_z(held, plane_wanted)
    incoming = lax.all_to_all(outgoing, ("x", "y", "c"), 0, 0, tiled=True)

    part, rounded, own_k, credit, credit_k = pair_weights(embeddings, incoming)
    credit = credit.reshape(PLANE * NBD, W)
    back = lax.all_to_all(credit, ("x", "y", "c"), 0, 0, tiled=True)
    back, own = lax.optimization_barrier((back, own_sums(rounded, part)))
    own_w = lax.psum_scatter(own, "x", tiled=True)[0]

    per_slot = jnp.sum(credit_k, axis=1).astype(BF16).reshape(BR, NBD)
    every = jnp.arange(KEYS * NBLK, dtype=jnp.int32)
    spread_k = (wanted[:, None] == every[None, :]).astype(BF16)
    dense_k = jnp.dot(per_slot, spread_k, preferred_element_type=F32)
    dense_k = dense_k.reshape(BR, NZ, PIECES * NBLK).transpose(1, 0, 2)
    plane_k = lax.psum_scatter(dense_k, "z", tiled=True)[0]

    got, got_k = sum_over_z(back, plane_wanted, plane_k)
    got_k = got_k + own_k.reshape(SLAB)
    got, own_w, got_k = lax.optimization_barrier((got, own_w, got_k))
    scale = 1.0 + lax.psum(got_k, "x")
    got = lax.all_to_all(got, ("y", "c"), 0, 0, tiled=True)
    rows = jnp.arange(SLAB, dtype=jnp.int32)
    source = (rows % RP) * (SLAB // RP) + (rows % BR) // RP * NBLK + rows // BR
    got = got.reshape(PIECES * NBLK, W)
    got = jnp.concatenate([got[:, r * CX : (r + 1) * CX] for r in range(RP)])
    order = (source[:, None] == rows[None, :]).astype(BF16)
    total_w = own_w.astype(F32) + jnp.dot(order, got, preferred_element_type=F32)
    mean = ((columns.astype(F32) + total_w) / scale[:, None]).astype(BF16)
    return jnp.log(scale), gather_over_x(lax.optimization_barrier(mean))


def solution(mesh):
    fine = Mesh(mesh.devices.reshape(NZ, NY, NC, NX), ("z", "y", "c", "x"))
    key = ("z", "y", "c")
    in_specs = (P(key, None), P(key, "x", None), P(key, "x"))
    out_specs = (P(key), P(key, None))
    return jax.shard_map(local, mesh=fine, in_specs=in_specs, out_specs=out_specs, check_vma=False)
```

```python
import jax
import jax.numpy as jnp
from jax import lax
from jax.experimental import pallas as pl
from jax.experimental.pallas import tpu as pltpu
from jax.sharding import Mesh, PartitionSpec as P

D = 1024
SLAB = 1024
BR = 16
NBLK = SLAB // BR
NBD = 64
KEYS = 64
NZ, NY, NC, NX = 8, 4, 2, 4
PIECES = NY * NC
RP = BR // PIECES
CX = D // NX
W = RP * CX
PLANE = NX * NY * NC
XBLK = NBLK // NX
LIST = 2 * NBD
TEMP = 0.05

F32, BF16 = jnp.float32, jnp.bfloat16
NT = (((1,), (1,)), ((), ()))
TN = (((0,), (0,)), ((), ()))


def pair_kernel(emb_ref, inc_ref, part_ref, rounded_ref, ownk_ref, cred_ref, credk_ref):
    emb = emb_ref[...]
    group = NC * RP * NBD
    for y in range(NY):
        for c in range(NC):
            for r in range(RP):
                for x in range(NX):
                    part_ref[pl.ds(y * group + (c * RP + r) * NBD, NBD), pl.ds(x * CX, CX)] = inc_ref[
                        x, NC * y + c, :, pl.ds(r * CX, CX)
                    ]
        part = part_ref[pl.ds(y * group, group), :]
        cosine = lax.dot_general(part, emb, NT, preferred_element_type=F32)
        weight = jnp.exp((cosine - 1.0) * (1.0 / TEMP))
        rounded = weight.astype(BF16)
        rounded_ref[pl.ds(y * group, group), :] = rounded
        ownk = jnp.sum(weight, axis=0, keepdims=True)
        if y == 0:
            ownk_ref[...] = ownk
        else:
            ownk_ref[...] += ownk
        credk_ref[pl.ds(y * group, group), :] = sum(weight[:, n : n + 128] for n in range(0, SLAB, 128))
        cred = jnp.dot(rounded, emb, preferred_element_type=F32).astype(BF16)
        for c in range(NC):
            for r in range(RP):
                at = (c * RP + r) * NBD
                for x in range(NX):
                    cred_ref[x, NC * y + c, :, pl.ds(r * CX, CX)] = cred[
                        at : at + NBD, x * CX : (x + 1) * CX
                    ]


def pair_weights(emb, inc):
    return pl.pallas_call(
        pair_kernel,
        out_shape=(
            pltpu.HBM((SLAB, D), BF16),
            pltpu.HBM((SLAB, SLAB), BF16),
            jax.ShapeDtypeStruct((1, SLAB), F32),
            pltpu.HBM((NX, PIECES, NBD, W), BF16),
            jax.ShapeDtypeStruct((SLAB, 128), F32),
        ),
        compiler_params=pltpu.CompilerParams(vmem_limit_bytes=20 << 20),
        cost_estimate=pl.CostEstimate(
            flops=4 * SLAB * SLAB * D, bytes_accessed=10 << 20, transcendentals=SLAB * SLAB
        ),
    )(emb, inc.reshape(NX, PIECES, NBD, W))


def own_kernel(rounded_ref, part_ref, own_ref):
    own = lax.dot_general(rounded_ref[...], part_ref[...], TN, preferred_element_type=F32)
    own_ref[0] = own.astype(BF16)


def own_sums(rounded, part):
    return pl.pallas_call(
        own_kernel,
        grid=(NX,),
        out_shape=pltpu.HBM((NX, SLAB, CX), BF16),
        in_specs=[
            pl.BlockSpec((SLAB, SLAB), lambda x: (0, 0)),
            pl.BlockSpec((SLAB, CX), lambda x: (0, x)),
        ],
        out_specs=pl.BlockSpec((1, SLAB, CX), lambda x: (x, 0, 0)),
        compiler_params=pltpu.CompilerParams(vmem_limit_bytes=12 << 20),
        cost_estimate=pl.CostEstimate(
            flops=2 * SLAB * SLAB * D, bytes_accessed=6 << 20, transcendentals=0
        ),
    )(*[pltpu.with_memory_space_constraint(a, pltpu.HBM) for a in (rounded, part)])


def shift(axis, by):
    n = lax.axis_size(axis)
    return [(i, (i + by) % n) for i in range(n)]


def up(a, axis):
    return lax.ppermute(a, axis, shift(axis, 1))


def down(a, axis):
    return lax.ppermute(a, axis, shift(axis, -1))


def gather_over_x(mine):
    me = lax.axis_index("x")
    half = SLAB // 2
    parts = [mine[:half], mine[half:]]
    ups = [up(p, "x") for p in parts]
    downs = [down(p, "x") for p in parts]
    far = [up(ups[0], "x"), down(downs[1], "x")]
    place = lambda out, a, row, k: lax.dynamic_update_slice(
        out, a, (row, lax.rem(me + k, NX) * CX)
    )
    out = jnp.concatenate([mine] * NX, axis=1)
    for p in range(2):
        out = place(out, ups[p], p * half, 3)
        out = place(out, downs[p], p * half, 1)
        out = place(out, far[p], p * half, 2)
    return out


def share_in_plane(embeddings, source, block):
    mine = lax.dynamic_slice_in_dim(embeddings, lax.axis_index("x") * (SLAB // NX), SLAB // NX, axis=0)
    rows = jnp.arange(SLAB // NX, dtype=jnp.int32)
    half = PIECES * XBLK
    origin = rows % XBLK * BR + rows % half // XBLK * RP + rows // half
    order = (origin[:, None] == rows[None, :]).astype(BF16)
    mine = jnp.dot(order, mine, preferred_element_type=F32).astype(BF16)
    lists = jnp.broadcast_to(jnp.concatenate([source, block]).astype(BF16), (half, LIST))
    sent = [
        jnp.concatenate([mine[:half, at : at + CX], mine[half:, at : at + CX], lists], axis=1)
        for at in range(0, D, CX)
    ]
    sent = jnp.concatenate(sent).reshape(PLANE, XBLK, W + LIST)
    got = lax.all_to_all(sent, ("x", "y", "c"), 0, 0, tiled=True)
    lists = got[:, 0, W:].astype(jnp.int32)
    source, block = lists[:, :NBD].reshape(-1), lists[:, NBD:].reshape(-1)
    row = ((block // XBLK) * PIECES + source % PIECES) * XBLK + block % XBLK
    return got[:, :, :W].reshape(PLANE * XBLK, W), (source // PIECES) * (PLANE * XBLK) + row


def pick_over_z(held, plane_wanted):
    me = lax.axis_index("z")
    rows = held.shape[0]
    half = rows // 2
    inside = jnp.arange(rows, dtype=jnp.int32)
    picked = None

    def take(picked, parts):
        at = jnp.concatenate(
            [lax.rem(me + k, NZ) * rows + inside[first : first + t.shape[0]] for k, first, t in parts]
        )
        pick = (plane_wanted[:, None] == at[None, :]).astype(BF16)
        got = jnp.dot(pick, jnp.concatenate([t for _, _, t in parts]), preferred_element_type=F32)
        return (got if picked is None else got + picked.astype(F32)).astype(BF16)

    ups = downs = [held[:half], held[half:]]
    picked = take(None, [(0, 0, held)])
    for step in range(1, NZ // 2):
        ups = [up(t, "z") for t in ups]
        downs = [down(t, "z") for t in downs]
        picked = take(
            picked,
            [(NZ - step, p * half, ups[p]) for p in range(2)]
            + [(step, p * half, downs[p]) for p in range(2)],
        )
    far = [(NZ // 2, 0, up(ups[0], "z")), (NZ // 2, half, down(downs[1], "z"))]
    return take(picked, far)


def credit_kernel(at_ref, wanted_ref, back_ref, *refs):
    n_out = at_ref.shape[0]
    arrived, outs = refs[:-n_out], refs[-n_out:]
    each = len(arrived) // n_out
    rows = outs[0].shape[0]
    iota = lax.broadcasted_iota(jnp.int32, (rows, PLANE * NBD), 0)
    spread = jnp.concatenate(
        [jnp.where(at_ref[i] + iota == wanted_ref[...], 1.0, 0.0).astype(BF16) for i in range(n_out)]
    )
    total = jnp.dot(spread, back_ref[...], preferred_element_type=F32)
    for i, out_ref in enumerate(outs):
        sums = total[i * rows : (i + 1) * rows]
        for a in arrived[i * each : (i + 1) * each]:
            sums += a[...].astype(F32)
        out_ref[...] = sums.astype(BF16)


def credit_sums(at, wanted, back, arrived):
    rows = PIECES * NBLK // 2
    vmem = pl.BlockSpec(memory_space=pltpu.VMEM)
    n_out = len(at)
    return pl.pallas_call(
        credit_kernel,
        out_shape=(jax.ShapeDtypeStruct((rows, W), BF16),) * n_out,
        in_specs=[pl.BlockSpec(memory_space=pltpu.SMEM)] + [vmem] * (2 + len(arrived)),
        out_specs=(vmem,) * n_out,
        compiler_params=pltpu.CompilerParams(vmem_limit_bytes=12 << 20),
        cost_estimate=pl.CostEstimate(
            flops=2 * n_out * rows * PLANE * NBD * W, bytes_accessed=3 << 20, transcendentals=0
        ),
    )(jnp.stack(at), wanted, back, *arrived)


def exchange_k(plane_k):
    all_k = lax.all_to_all(plane_k.reshape(BR, PIECES, NBLK), ("y", "c"), 1, 0, tiled=True)
    return jnp.sum(all_k.reshape(PIECES, BR, NBLK), axis=0).T.reshape(SLAB)


def sum_over_z(back, plane_wanted, later):
    me = lax.axis_index("z")
    rows = PIECES * NBLK
    wanted = plane_wanted[None, :]

    def sums(targets, arrived=()):
        at = [lax.rem(me + k, NZ) * rows + part * (rows // 2) for k, part in targets]
        return credit_sums(at, wanted, back, arrived)

    far = NZ // 2
    first = sums([(far, 0), (far, 1)])
    ups, downs = [up(first[0], "z"), None], [None, down(first[1], "z")]
    second = sums([(far - 1, 1), (far + 1, 0)])
    ups[1], downs[0] = up(second[0], "z"), down(second[1], "z")
    third = sums([(far - 1, 0), (far + 1, 1)], [ups[0], downs[1]])
    ups[0], downs[1] = up(third[0], "z"), down(third[1], "z")
    ups[1], later = lax.optimization_barrier((ups[1], later))
    for k in range(far - 2, 0, -1):
        for p in range(2):
            sent = sums([(k, 1 - p), (NZ - k, p)], [ups[1 - p], downs[p]])
            ups[1 - p], downs[p] = up(sent[0], "z"), down(sent[1], "z")
    last = [sums([(0, p)], [ups[p], downs[p]])[0] for p in range(2)]
    return jnp.concatenate(last), later


def local(embeddings, sources, blocks):
    me_x = lax.axis_index("x")
    source, block = sources[0, :, 0], blocks[0]
    held, plane_wanted = share_in_plane(embeddings, source, block)
    outgoing = pick_over_z(held, plane_wanted)
    incoming = lax.all_to_all(outgoing, ("x", "y", "c"), 0, 0, tiled=True)

    part, rounded, own_k, credit, credit_k = pair_weights(embeddings, incoming)
    credit = credit.reshape(PLANE * NBD, W)
    back = lax.all_to_all(credit, ("x", "y", "c"), 0, 0, tiled=True)
    back, own = lax.optimization_barrier((back, own_sums(rounded, part)))
    own_w = lax.psum_scatter(own, "x", tiled=True)[0]

    per_slot = jnp.sum(credit_k, axis=1).astype(BF16).reshape(BR, NBD)
    every = jnp.arange(KEYS * NBLK, dtype=jnp.int32)
    spread_k = ((source * NBLK + block)[:, None] == every[None, :]).astype(BF16)
    dense_k = jnp.dot(per_slot, spread_k, preferred_element_type=F32)
    dense_k = dense_k.reshape(BR, NZ, PIECES * NBLK).transpose(1, 0, 2)
    plane_k = lax.psum_scatter(dense_k, "z", tiled=True)[0]

    got, plane_k = sum_over_z(back, plane_wanted, plane_k)
    got_k = exchange_k(plane_k) + own_k.reshape(SLAB)
    got, own_w, got_k = lax.optimization_barrier((got, own_w, got_k))
    scale = 1.0 + lax.psum(got_k, "x")
    got = got.reshape(NX, PIECES, XBLK, W).transpose(1, 0, 2, 3).reshape(PIECES * NBLK, W)
    got = lax.all_to_all(got, ("y", "c"), 0, 0, tiled=True)
    rows = jnp.arange(SLAB, dtype=jnp.int32)
    origin = (rows % RP) * (SLAB // RP) + (rows % BR) // RP * NBLK + rows // BR
    got = got.reshape(PIECES * NBLK, W)
    got = jnp.concatenate([got[:, r * CX : (r + 1) * CX] for r in range(RP)])
    order = (origin[:, None] == rows[None, :]).astype(BF16)
    columns = lax.dynamic_slice_in_dim(embeddings, me_x * CX, CX, axis=1)
    total_w = own_w.astype(F32) + jnp.dot(order, got, preferred_element_type=F32)
    mean = ((columns.astype(F32) + total_w) / scale[:, None]).astype(BF16)
    return jnp.log(scale), gather_over_x(lax.optimization_barrier(mean))


def solution(mesh):
    fine = Mesh(mesh.devices.reshape(NZ, NY, NC, NX), ("z", "y", "c", "x"))
    key = ("z", "y", "c")
    in_specs = (P(key, None), P(key, "x", None), P(key, "x"))
    out_specs = (P(key), P(key, None))
    return jax.shard_map(local, mesh=fine, in_specs=in_specs, out_specs=out_specs, check_vma=False)
```

```python
import functools

import jax
import jax.numpy as jnp
from jax import lax
from jax.experimental import pallas as pl
from jax.experimental.pallas import tpu as pltpu
from jax.sharding import Mesh, PartitionSpec as P

D = 1024
SLAB = 1024
BR = 16
NBLK = SLAB // BR
NBD = 64
KEYS = 64
NZ, NY, NC, NX = 8, 4, 2, 4
PIECES = NY * NC
RP = BR // PIECES
CX = D // NX
W = RP * CX
PLANE = NX * NY * NC
XBLK = NBLK // NX
LIST = 2 * NBD
TEMP = 0.05

F32, BF16 = jnp.float32, jnp.bfloat16
NT = (((1,), (1,)), ((), ()))
TN = (((0,), (0,)), ((), ()))


def pair_kernel(emb_ref, inc_ref, part_ref, rounded_ref, ownk_ref, cred_ref, credk_ref):
    emb = emb_ref[...]
    group = NC * RP * NBD
    for y in range(NY):
        for c in range(NC):
            for r in range(RP):
                for x in range(NX):
                    part_ref[pl.ds(y * group + (c * RP + r) * NBD, NBD), pl.ds(x * CX, CX)] = inc_ref[
                        x, NC * y + c, :, pl.ds(r * CX, CX)
                    ]
        part = part_ref[pl.ds(y * group, group), :]
        cosine = lax.dot_general(part, emb, NT, preferred_element_type=F32)
        weight = jnp.exp((cosine - 1.0) * (1.0 / TEMP))
        rounded = weight.astype(BF16)
        rounded_ref[pl.ds(y * group, group), :] = rounded
        ownk = jnp.sum(weight, axis=0, keepdims=True)
        if y == 0:
            ownk_ref[...] = ownk
        else:
            ownk_ref[...] += ownk
        credk_ref[pl.ds(y * group, group), :] = sum(weight[:, n : n + 128] for n in range(0, SLAB, 128))
        cred = jnp.dot(rounded, emb, preferred_element_type=F32).astype(BF16)
        for c in range(NC):
            for r in range(RP):
                at = (c * RP + r) * NBD
                for x in range(NX):
                    cred_ref[x, NC * y + c, :, pl.ds(r * CX, CX)] = cred[
                        at : at + NBD, x * CX : (x + 1) * CX
                    ]


def pair_weights(emb, inc):
    return pl.pallas_call(
        pair_kernel,
        out_shape=(
            pltpu.HBM((SLAB, D), BF16),
            pltpu.HBM((SLAB, SLAB), BF16),
            jax.ShapeDtypeStruct((1, SLAB), F32),
            pltpu.HBM((NX, PIECES, NBD, W), BF16),
            jax.ShapeDtypeStruct((SLAB, 128), F32),
        ),
        compiler_params=pltpu.CompilerParams(vmem_limit_bytes=20 << 20),
        cost_estimate=pl.CostEstimate(
            flops=4 * SLAB * SLAB * D, bytes_accessed=10 << 20, transcendentals=SLAB * SLAB
        ),
    )(emb, inc.reshape(NX, PIECES, NBD, W))


def own_kernel(rounded_ref, part_ref, own_ref):
    own = lax.dot_general(rounded_ref[...], part_ref[...], TN, preferred_element_type=F32)
    own_ref[0] = own.astype(BF16)


def own_sums(rounded, part):
    return pl.pallas_call(
        own_kernel,
        grid=(NX,),
        out_shape=pltpu.HBM((NX, SLAB, CX), BF16),
        in_specs=[
            pl.BlockSpec((SLAB, SLAB), lambda x: (0, 0)),
            pl.BlockSpec((SLAB, CX), lambda x: (0, x)),
        ],
        out_specs=pl.BlockSpec((1, SLAB, CX), lambda x: (x, 0, 0)),
        compiler_params=pltpu.CompilerParams(vmem_limit_bytes=12 << 20),
        cost_estimate=pl.CostEstimate(
            flops=2 * SLAB * SLAB * D, bytes_accessed=6 << 20, transcendentals=0
        ),
    )(*[pltpu.with_memory_space_constraint(a, pltpu.HBM) for a in (rounded, part)])


def shift(axis, by):
    n = lax.axis_size(axis)
    return [(i, (i + by) % n) for i in range(n)]


def up(a, axis):
    return lax.ppermute(a, axis, shift(axis, 1))


def down(a, axis):
    return lax.ppermute(a, axis, shift(axis, -1))


def gather_over_x(mine):
    me = lax.axis_index("x")
    half = SLAB // 2
    parts = [mine[:half], mine[half:]]
    ups = [up(p, "x") for p in parts]
    downs = [down(p, "x") for p in parts]
    far = [up(ups[0], "x"), down(downs[1], "x")]
    place = lambda out, a, row, k: lax.dynamic_update_slice(
        out, a, (row, lax.rem(me + k, NX) * CX)
    )
    out = jnp.concatenate([mine] * NX, axis=1)
    for p in range(2):
        out = place(out, ups[p], p * half, 3)
        out = place(out, downs[p], p * half, 1)
        out = place(out, far[p], p * half, 2)
    return out


def share_in_plane(embeddings, source, block):
    mine = lax.dynamic_slice_in_dim(embeddings, lax.axis_index("x") * (SLAB // NX), SLAB // NX, axis=0)
    rows = jnp.arange(SLAB // NX, dtype=jnp.int32)
    half = PIECES * XBLK
    origin = rows % XBLK * BR + rows % half // XBLK * RP + rows // half
    order = (origin[:, None] == rows[None, :]).astype(BF16)
    mine = jnp.dot(order, mine, preferred_element_type=F32).astype(BF16)
    lists = jnp.broadcast_to(jnp.concatenate([source, block]).astype(BF16), (half, LIST))
    sent = [
        jnp.concatenate([mine[:half, at : at + CX], mine[half:, at : at + CX], lists], axis=1)
        for at in range(0, D, CX)
    ]
    sent = jnp.concatenate(sent).reshape(PLANE, XBLK, W + LIST)
    got = lax.all_to_all(sent, ("x", "y", "c"), 0, 0, tiled=True)
    lists = got[:, 0, W:].astype(jnp.int32)
    source, block = lists[:, :NBD].reshape(-1), lists[:, NBD:].reshape(-1)
    row = ((block // XBLK) * PIECES + source % PIECES) * XBLK + block % XBLK
    return got[:, :, :W].reshape(PLANE * XBLK, W), (source // PIECES) * (PLANE * XBLK) + row


def pick_over_z(held, plane_wanted):
    me = lax.axis_index("z")
    rows = held.shape[0]
    half = rows // 2
    inside = jnp.arange(rows, dtype=jnp.int32)
    picked = None

    def take(picked, parts):
        at = jnp.concatenate(
            [lax.rem(me + k, NZ) * rows + inside[first : first + t.shape[0]] for k, first, t in parts]
        )
        pick = (plane_wanted[:, None] == at[None, :]).astype(BF16)
        got = jnp.dot(pick, jnp.concatenate([t for _, _, t in parts]), preferred_element_type=F32)
        return (got if picked is None else got + picked.astype(F32)).astype(BF16)

    ups = downs = [held[:half], held[half:]]
    picked = take(None, [(0, 0, held)])
    for step in range(1, NZ // 2):
        ups = [up(t, "z") for t in ups]
        downs = [down(t, "z") for t in downs]
        picked = take(
            picked,
            [(NZ - step, p * half, ups[p]) for p in range(2)]
            + [(step, p * half, downs[p]) for p in range(2)],
        )
    far = [(NZ // 2, 0, up(ups[0], "z")), (NZ // 2, half, down(downs[1], "z"))]
    return take(picked, far)


def credit_kernel(targets, first_ref, wanted_ref, back_ref, *refs):
    n_out = len(targets)
    refs, (in_ref, sum_ref, in_sems, out_sems) = refs[:-4], refs[-4:]
    arrived, outs = refs[:-n_out], refs[-n_out:]
    each = len(arrived) // n_out
    rows = outs[0].shape[0]
    loads = [pltpu.make_async_copy(a, in_ref.at[n], in_sems.at[n]) for n, a in enumerate(arrived)]
    stores = [pltpu.make_async_copy(sum_ref.at[i], o, out_sems.at[i]) for i, o in enumerate(outs)]
    for load in loads:
        load.start()
    iota = lax.broadcasted_iota(jnp.int32, (rows, PLANE * NBD), 0)
    for i, (k, part) in enumerate(targets):
        row = first_ref[k] + part * rows + iota
        spread = jnp.where(row == wanted_ref[...], 1.0, 0.0).astype(BF16)
        total = jnp.dot(spread, back_ref[...], preferred_element_type=F32)
        for n in range(i * each, (i + 1) * each):
            loads[n].wait()
            total += in_ref[n].astype(F32)
        sum_ref[i] = total.astype(BF16)
        stores[i].start()
    for store in stores:
        store.wait()


def credit_sums(targets, first, wanted, back, arrived):
    rows = PIECES * NBLK // 2
    vmem, anywhere = pl.BlockSpec(memory_space=pltpu.VMEM), pl.BlockSpec(memory_space=pl.ANY)
    n_out, n_in = len(targets), max(1, len(arrived))
    return pl.pallas_call(
        functools.partial(credit_kernel, targets),
        out_shape=(jax.ShapeDtypeStruct((rows, W), BF16),) * n_out,
        in_specs=[pl.BlockSpec(memory_space=pltpu.SMEM), vmem, vmem] + [anywhere] * len(arrived),
        out_specs=(anywhere,) * n_out,
        scratch_shapes=[
            pltpu.VMEM((n_in, rows, W), BF16),
            pltpu.VMEM((n_out, rows, W), BF16),
            pltpu.SemaphoreType.DMA((n_in,)),
            pltpu.SemaphoreType.DMA((n_out,)),
        ],
        compiler_params=pltpu.CompilerParams(vmem_limit_bytes=12 << 20),
        cost_estimate=pl.CostEstimate(
            flops=2 * n_out * rows * PLANE * NBD * W, bytes_accessed=3 << 20, transcendentals=0
        ),
    )(first, wanted, back, *arrived)


def exchange_k(plane_k):
    all_k = lax.all_to_all(plane_k.reshape(BR, PIECES, NBLK), ("y", "c"), 1, 0, tiled=True)
    return jnp.sum(all_k.reshape(PIECES, BR, NBLK), axis=0).T.reshape(SLAB)


def first_rows():
    far = lax.axis_index("z") + jnp.arange(NZ, dtype=jnp.int32)
    return lax.rem(far, NZ) * (PIECES * NBLK)


def sum_over_z(back, wanted, first, later):
    def sums(targets, arrived=()):
        return credit_sums(tuple(targets), first, wanted, back, arrived)

    far = NZ // 2
    sent = sums([(far, 0), (far, 1)])
    ups, downs = [up(sent[0], "z"), None], [None, down(sent[1], "z")]
    second = sums([(far - 1, 1), (far + 1, 0)])
    ups[1], downs[0] = up(second[0], "z"), down(second[1], "z")
    third = sums([(far - 1, 0), (far + 1, 1)], [ups[0], downs[1]])
    ups[0], downs[1] = up(third[0], "z"), down(third[1], "z")
    ups[1], later = lax.optimization_barrier((ups[1], later))
    for k in range(far - 2, 0, -1):
        for p in range(2):
            sent = sums([(k, 1 - p), (NZ - k, p)], [ups[1 - p], downs[p]])
            ups[1 - p], downs[p] = up(sent[0], "z"), down(sent[1], "z")
    last = [sums([(0, p)], [ups[p], downs[p]])[0] for p in range(2)]
    return jnp.concatenate(last), later


def local(embeddings, sources, blocks):
    me_x = lax.axis_index("x")
    source, block = sources[0, :, 0], blocks[0]
    held, plane_wanted = share_in_plane(embeddings, source, block)
    outgoing = pick_over_z(held, plane_wanted)
    incoming = lax.all_to_all(outgoing, ("x", "y", "c"), 0, 0, tiled=True)

    part, rounded, own_k, credit, credit_k = pair_weights(embeddings, incoming)
    credit = credit.reshape(PLANE * NBD, W)
    back = lax.all_to_all(credit, ("x", "y", "c"), 0, 0, tiled=True)
    columns = lax.dynamic_slice_in_dim(embeddings, me_x * CX, CX, axis=1)
    wanted, first = plane_wanted[None, :], first_rows()
    back, own, columns, wanted, first = lax.optimization_barrier(
        (back, own_sums(rounded, part), columns, wanted, first)
    )
    own_w = lax.psum_scatter(own, "x", tiled=True)[0]

    per_slot = jnp.sum(credit_k, axis=1).astype(BF16).reshape(BR, NBD)
    every = jnp.arange(KEYS * NBLK, dtype=jnp.int32)
    spread_k = ((source * NBLK + block)[:, None] == every[None, :]).astype(BF16)
    dense_k = jnp.dot(per_slot, spread_k, preferred_element_type=F32)
    dense_k = dense_k.reshape(BR, NZ, PIECES * NBLK).transpose(1, 0, 2)
    plane_k = lax.psum_scatter(dense_k, "z", tiled=True)[0]

    got, plane_k = sum_over_z(back, wanted, first, plane_k)
    got_k = exchange_k(plane_k) + own_k.reshape(SLAB)
    got, own_w, got_k = lax.optimization_barrier((got, own_w, got_k))
    scale = 1.0 + lax.psum(got_k, "x")
    got = got.reshape(NX, PIECES, XBLK, W).transpose(1, 0, 2, 3).reshape(PIECES * NBLK, W)
    got = lax.all_to_all(got, ("y", "c"), 0, 0, tiled=True)
    rows = jnp.arange(SLAB, dtype=jnp.int32)
    origin = (rows % RP) * (SLAB // RP) + (rows % BR) // RP * NBLK + rows // BR
    got = got.reshape(PIECES * NBLK, W)
    got = jnp.concatenate([got[:, r * CX : (r + 1) * CX] for r in range(RP)])
    order = (origin[:, None] == rows[None, :]).astype(BF16)
    total_w = own_w.astype(F32) + jnp.dot(order, got, preferred_element_type=F32)
    mean = ((columns.astype(F32) + total_w) / scale[:, None]).astype(BF16)
    return jnp.log(scale), gather_over_x(lax.optimization_barrier(mean))


def solution(mesh):
    fine = Mesh(mesh.devices.reshape(NZ, NY, NC, NX), ("z", "y", "c", "x"))
    key = ("z", "y", "c")
    in_specs = (P(key, None), P(key, "x", None), P(key, "x"))
    out_specs = (P(key), P(key, None))
    return jax.shard_map(local, mesh=fine, in_specs=in_specs, out_specs=out_specs, check_vma=False)
```

```python
import functools

import jax
import jax.numpy as jnp
from jax import lax
from jax.experimental import pallas as pl
from jax.experimental.pallas import tpu as pltpu
from jax.sharding import Mesh, PartitionSpec as P

D = 1024
SLAB = 1024
BR = 16
NBLK = SLAB // BR
NBD = 64
KEYS = 64
NZ, NY, NC, NX = 8, 4, 2, 4
PIECES = NY * NC
RP = BR // PIECES
CX = D // NX
W = RP * CX
PLANE = NX * NY * NC
XBLK = NBLK // NX
LIST = 2 * NBD
TEMP = 0.05

F32, BF16 = jnp.float32, jnp.bfloat16
NT = (((1,), (1,)), ((), ()))
TN = (((0,), (0,)), ((), ()))


def pair_kernel(emb_ref, inc_any, part_any, rounded_any, ownk_ref, cred_any, credk_ref, *scratch):
    inc_ref, part_ref, rounded_ref, cred_ref, in_sems, out_sems = scratch
    group = NC * RP * NBD
    loads, stores = [], []
    for y in range(NY):
        pieces, rows = pl.ds(NC * y, NC), pl.ds(y * group, group)
        loads.append(pltpu.make_async_copy(inc_any.at[:, pieces], inc_ref.at[:, pieces], in_sems.at[y]))
        stores.append(
            [
                pltpu.make_async_copy(part_ref.at[rows], part_any.at[rows], out_sems.at[0, y]),
                pltpu.make_async_copy(rounded_ref.at[rows], rounded_any.at[rows], out_sems.at[1, y]),
                pltpu.make_async_copy(cred_ref.at[:, pieces], cred_any.at[:, pieces], out_sems.at[2, y]),
            ]
        )
        loads[y].start()
    emb = emb_ref[...]
    for y in range(NY):
        loads[y].wait()
        for c in range(NC):
            for r in range(RP):
                for x in range(NX):
                    part_ref[pl.ds(y * group + (c * RP + r) * NBD, NBD), pl.ds(x * CX, CX)] = inc_ref[
                        x, NC * y + c, :, pl.ds(r * CX, CX)
                    ]
        stores[y][0].start()
        part = part_ref[pl.ds(y * group, group), :]
        cosine = lax.dot_general(part, emb, NT, preferred_element_type=F32)
        weight = jnp.exp((cosine - 1.0) * (1.0 / TEMP))
        rounded = weight.astype(BF16)
        rounded_ref[pl.ds(y * group, group), :] = rounded
        stores[y][1].start()
        ownk = jnp.sum(weight, axis=0, keepdims=True)
        if y == 0:
            ownk_ref[...] = ownk
        else:
            ownk_ref[...] += ownk
        credk_ref[pl.ds(y * group, group), :] = sum(weight[:, n : n + 128] for n in range(0, SLAB, 128))
        cred = jnp.dot(rounded, emb, preferred_element_type=F32).astype(BF16)
        for c in range(NC):
            for r in range(RP):
                at = (c * RP + r) * NBD
                for x in range(NX):
                    cred_ref[x, NC * y + c, :, pl.ds(r * CX, CX)] = cred[
                        at : at + NBD, x * CX : (x + 1) * CX
                    ]
        stores[y][2].start()
    for y in range(NY):
        for store in stores[y]:
            store.wait()


def pair_weights(emb, inc):
    vmem, anywhere = pl.BlockSpec(memory_space=pltpu.VMEM), pl.BlockSpec(memory_space=pl.ANY)
    pieces = (NX, PIECES, NBD, W)
    return pl.pallas_call(
        pair_kernel,
        out_shape=(
            pltpu.HBM((SLAB, D), BF16),
            pltpu.HBM((SLAB, SLAB), BF16),
            jax.ShapeDtypeStruct((1, SLAB), F32),
            pltpu.HBM(pieces, BF16),
            jax.ShapeDtypeStruct((SLAB, 128), F32),
        ),
        in_specs=[vmem, anywhere],
        out_specs=(anywhere, anywhere, vmem, anywhere, vmem),
        scratch_shapes=[
            pltpu.VMEM(pieces, BF16),
            pltpu.VMEM((SLAB, D), BF16),
            pltpu.VMEM((SLAB, SLAB), BF16),
            pltpu.VMEM(pieces, BF16),
            pltpu.SemaphoreType.DMA((NY,)),
            pltpu.SemaphoreType.DMA((3, NY)),
        ],
        compiler_params=pltpu.CompilerParams(vmem_limit_bytes=20 << 20),
        cost_estimate=pl.CostEstimate(
            flops=4 * SLAB * SLAB * D, bytes_accessed=10 << 20, transcendentals=SLAB * SLAB
        ),
    )(emb, inc.reshape(pieces))


def own_kernel(rounded_ref, part_ref, own_ref):
    own = lax.dot_general(rounded_ref[...], part_ref[...], TN, preferred_element_type=F32)
    own_ref[0] = own.astype(BF16)


def own_sums(rounded, part):
    return pl.pallas_call(
        own_kernel,
        grid=(NX,),
        out_shape=pltpu.HBM((NX, SLAB, CX), BF16),
        in_specs=[
            pl.BlockSpec((SLAB, SLAB), lambda x: (0, 0)),
            pl.BlockSpec((SLAB, CX), lambda x: (0, x)),
        ],
        out_specs=pl.BlockSpec((1, SLAB, CX), lambda x: (x, 0, 0)),
        compiler_params=pltpu.CompilerParams(vmem_limit_bytes=12 << 20),
        cost_estimate=pl.CostEstimate(
            flops=2 * SLAB * SLAB * D, bytes_accessed=6 << 20, transcendentals=0
        ),
    )(*[pltpu.with_memory_space_constraint(a, pltpu.HBM) for a in (rounded, part)])


def shift(axis, by):
    n = lax.axis_size(axis)
    return [(i, (i + by) % n) for i in range(n)]


def up(a, axis):
    return lax.ppermute(a, axis, shift(axis, 1))


def down(a, axis):
    return lax.ppermute(a, axis, shift(axis, -1))


def gather_over_x(mine):
    me = lax.axis_index("x")
    half = SLAB // 2
    parts = [mine[:half], mine[half:]]
    ups = [up(p, "x") for p in parts]
    downs = [down(p, "x") for p in parts]
    far = [up(ups[0], "x"), down(downs[1], "x")]
    place = lambda out, a, row, k: lax.dynamic_update_slice(
        out, a, (row, lax.rem(me + k, NX) * CX)
    )
    out = jnp.concatenate([mine] * NX, axis=1)
    for p in range(2):
        out = place(out, ups[p], p * half, 3)
        out = place(out, downs[p], p * half, 1)
        out = place(out, far[p], p * half, 2)
    return out


def share_in_plane(embeddings, source, block):
    mine = lax.dynamic_slice_in_dim(embeddings, lax.axis_index("x") * (SLAB // NX), SLAB // NX, axis=0)
    rows = jnp.arange(SLAB // NX, dtype=jnp.int32)
    half = PIECES * XBLK
    origin = rows % XBLK * BR + rows % half // XBLK * RP + rows // half
    order = (origin[:, None] == rows[None, :]).astype(BF16)
    mine = jnp.dot(order, mine, preferred_element_type=F32).astype(BF16)
    lists = jnp.broadcast_to(jnp.concatenate([source, block]).astype(BF16), (half, LIST))
    sent = [
        jnp.concatenate([mine[:half, at : at + CX], mine[half:, at : at + CX], lists], axis=1)
        for at in range(0, D, CX)
    ]
    sent = jnp.concatenate(sent).reshape(PLANE, XBLK, W + LIST)
    got = lax.all_to_all(sent, ("x", "y", "c"), 0, 0, tiled=True)
    lists = got[:, 0, W:].astype(jnp.int32)
    source, block = lists[:, :NBD].reshape(-1), lists[:, NBD:].reshape(-1)
    row = ((block // XBLK) * PIECES + source % PIECES) * XBLK + block % XBLK
    return got[:, :, :W].reshape(PLANE * XBLK, W), (source // PIECES) * (PLANE * XBLK) + row


def pick_over_z(held, plane_wanted):
    me = lax.axis_index("z")
    rows = held.shape[0]
    half = rows // 2
    inside = jnp.arange(rows, dtype=jnp.int32)
    picked = None

    def take(picked, parts):
        at = jnp.concatenate(
            [lax.rem(me + k, NZ) * rows + inside[first : first + t.shape[0]] for k, first, t in parts]
        )
        pick = (plane_wanted[:, None] == at[None, :]).astype(BF16)
        got = jnp.dot(pick, jnp.concatenate([t for _, _, t in parts]), preferred_element_type=F32)
        return (got if picked is None else got + picked.astype(F32)).astype(BF16)

    ups = downs = [held[:half], held[half:]]
    picked = take(None, [(0, 0, held)])
    for step in range(1, NZ // 2):
        ups = [up(t, "z") for t in ups]
        downs = [down(t, "z") for t in downs]
        picked = take(
            picked,
            [(NZ - step, p * half, ups[p]) for p in range(2)]
            + [(step, p * half, downs[p]) for p in range(2)],
        )
    far = [(NZ // 2, 0, up(ups[0], "z")), (NZ // 2, half, down(downs[1], "z"))]
    return take(picked, far)


def credit_kernel(targets, first_ref, wanted_ref, back_ref, *refs):
    n_out = len(targets)
    refs, (in_ref, sum_ref, in_sems, out_sems) = refs[:-4], refs[-4:]
    arrived, outs = refs[:-n_out], refs[-n_out:]
    each = len(arrived) // n_out
    rows = outs[0].shape[0]
    loads = [pltpu.make_async_copy(a, in_ref.at[n], in_sems.at[n]) for n, a in enumerate(arrived)]
    stores = [pltpu.make_async_copy(sum_ref.at[i], o, out_sems.at[i]) for i, o in enumerate(outs)]
    for load in loads:
        load.start()
    iota = lax.broadcasted_iota(jnp.int32, (rows, PLANE * NBD), 0)
    for i, (k, part) in enumerate(targets):
        row = first_ref[k] + part * rows + iota
        spread = jnp.where(row == wanted_ref[...], 1.0, 0.0).astype(BF16)
        total = jnp.dot(spread, back_ref[...], preferred_element_type=F32)
        for n in range(i * each, (i + 1) * each):
            loads[n].wait()
            total += in_ref[n].astype(F32)
        sum_ref[i] = total.astype(BF16)
        stores[i].start()
    for store in stores:
        store.wait()


def last_kernel(first_ref, wanted_ref, back_ref, *refs):
    arrived, (out_ref, in_ref, in_sems) = refs[:-3], refs[-3:]
    rows = PIECES * NBLK // 2
    loads = [pltpu.make_async_copy(a, in_ref.at[n], in_sems.at[n]) for n, a in enumerate(arrived)]
    for load in loads:
        load.start()
    iota = lax.broadcasted_iota(jnp.int32, (rows, PLANE * NBD), 0)
    for part in range(2):
        spread = jnp.where(first_ref[0] + part * rows + iota == wanted_ref[...], 1.0, 0.0).astype(BF16)
        total = jnp.dot(spread, back_ref[...], preferred_element_type=F32)
        for n in range(2 * part, 2 * part + 2):
            loads[n].wait()
            total += in_ref[n].astype(F32)
        total = total.astype(BF16)
        for n in range(NX // 2 * PIECES):
            x, piece = part * (NX // 2) + n // PIECES, n % PIECES
            out_ref[pl.ds((piece * NX + x) * XBLK, XBLK), :] = total[n * XBLK : (n + 1) * XBLK]


def last_sums(first, wanted, back, arrived):
    rows = PIECES * NBLK // 2
    vmem, anywhere = pl.BlockSpec(memory_space=pltpu.VMEM), pl.BlockSpec(memory_space=pl.ANY)
    return pl.pallas_call(
        last_kernel,
        out_shape=jax.ShapeDtypeStruct((2 * rows, W), BF16),
        in_specs=[pl.BlockSpec(memory_space=pltpu.SMEM), vmem, vmem] + [anywhere] * 4,
        out_specs=vmem,
        scratch_shapes=[pltpu.VMEM((4, rows, W), BF16), pltpu.SemaphoreType.DMA((4,))],
        compiler_params=pltpu.CompilerParams(vmem_limit_bytes=12 << 20),
        cost_estimate=pl.CostEstimate(
            flops=4 * rows * PLANE * NBD * W, bytes_accessed=3 << 20, transcendentals=0
        ),
    )(first, wanted, back, *arrived)


def credit_sums(targets, first, wanted, back, arrived):
    rows = PIECES * NBLK // 2
    vmem, anywhere = pl.BlockSpec(memory_space=pltpu.VMEM), pl.BlockSpec(memory_space=pl.ANY)
    n_out, n_in = len(targets), max(1, len(arrived))
    return pl.pallas_call(
        functools.partial(credit_kernel, targets),
        out_shape=(jax.ShapeDtypeStruct((rows, W), BF16),) * n_out,
        in_specs=[pl.BlockSpec(memory_space=pltpu.SMEM), vmem, vmem] + [anywhere] * len(arrived),
        out_specs=(anywhere,) * n_out,
        scratch_shapes=[
            pltpu.VMEM((n_in, rows, W), BF16),
            pltpu.VMEM((n_out, rows, W), BF16),
            pltpu.SemaphoreType.DMA((n_in,)),
            pltpu.SemaphoreType.DMA((n_out,)),
        ],
        compiler_params=pltpu.CompilerParams(vmem_limit_bytes=12 << 20),
        cost_estimate=pl.CostEstimate(
            flops=2 * n_out * rows * PLANE * NBD * W, bytes_accessed=3 << 20, transcendentals=0
        ),
    )(first, wanted, back, *arrived)


def exchange_k(plane_k):
    all_k = lax.all_to_all(plane_k.reshape(BR, PIECES, NBLK), ("y", "c"), 1, 0, tiled=True)
    return jnp.sum(all_k.reshape(PIECES, BR, NBLK), axis=0).T.reshape(SLAB)


def first_rows():
    far = lax.axis_index("z") + jnp.arange(NZ, dtype=jnp.int32)
    return lax.rem(far, NZ) * (PIECES * NBLK)


def sum_over_z(back, wanted, first, later):
    def sums(targets, arrived=()):
        return credit_sums(tuple(targets), first, wanted, back, arrived)

    far = NZ // 2
    sent = sums([(far, 0), (far, 1)])
    ups, downs = [up(sent[0], "z"), None], [None, down(sent[1], "z")]
    second = sums([(far - 1, 1), (far + 1, 0)])
    ups[1], downs[0] = up(second[0], "z"), down(second[1], "z")
    third = sums([(far - 1, 0), (far + 1, 1)], [ups[0], downs[1]])
    ups[0], downs[1] = up(third[0], "z"), down(third[1], "z")
    ups[1], later = lax.optimization_barrier((ups[1], later))
    for k in range(far - 2, 0, -1):
        for p in range(2):
            sent = sums([(k, 1 - p), (NZ - k, p)], [ups[1 - p], downs[p]])
            ups[1 - p], downs[p] = up(sent[0], "z"), down(sent[1], "z")
    return last_sums(first, wanted, back, [ups[0], downs[0], ups[1], downs[1]]), later


def local(embeddings, sources, blocks):
    me_x = lax.axis_index("x")
    source, block = sources[0, :, 0], blocks[0]
    held, plane_wanted = share_in_plane(embeddings, source, block)
    outgoing = pick_over_z(held, plane_wanted)
    incoming = lax.all_to_all(outgoing, ("x", "y", "c"), 0, 0, tiled=True)

    part, rounded, own_k, credit, credit_k = pair_weights(embeddings, incoming)
    credit = credit.reshape(PLANE * NBD, W)
    back = lax.all_to_all(credit, ("x", "y", "c"), 0, 0, tiled=True)
    columns = lax.dynamic_slice_in_dim(embeddings, me_x * CX, CX, axis=1)
    wanted, first = plane_wanted[None, :], first_rows()
    back, own, columns, wanted, first = lax.optimization_barrier(
        (back, own_sums(rounded, part), columns, wanted, first)
    )
    own_w = lax.psum_scatter(own, "x", tiled=True)[0]

    per_slot = jnp.sum(credit_k, axis=1).astype(BF16).reshape(BR, NBD)
    every = jnp.arange(KEYS * NBLK, dtype=jnp.int32)
    spread_k = ((source * NBLK + block)[:, None] == every[None, :]).astype(BF16)
    dense_k = jnp.dot(per_slot, spread_k, preferred_element_type=F32)
    dense_k = dense_k.reshape(BR, NZ, PIECES * NBLK).transpose(1, 0, 2)
    plane_k = lax.psum_scatter(dense_k, "z", tiled=True)[0]

    got, plane_k = sum_over_z(back, wanted, first, plane_k)
    got_k = exchange_k(plane_k) + own_k.reshape(SLAB)
    got, own_w, got_k = lax.optimization_barrier((got, own_w, got_k))
    scale = 1.0 + lax.psum(got_k, "x")
    got = lax.all_to_all(got, ("y", "c"), 0, 0, tiled=True)
    rows = jnp.arange(SLAB, dtype=jnp.int32)
    origin = (rows % RP) * (SLAB // RP) + (rows % BR) // RP * NBLK + rows // BR
    got = got.reshape(PIECES * NBLK, W)
    got = jnp.concatenate([got[:, r * CX : (r + 1) * CX] for r in range(RP)])
    order = (origin[:, None] == rows[None, :]).astype(BF16)
    total_w = own_w.astype(F32) + jnp.dot(order, got, preferred_element_type=F32)
    mean = ((columns.astype(F32) + total_w) / scale[:, None]).astype(BF16)
    return jnp.log(scale), gather_over_x(lax.optimization_barrier(mean))


def solution(mesh):
    fine = Mesh(mesh.devices.reshape(NZ, NY, NC, NX), ("z", "y", "c", "x"))
    key = ("z", "y", "c")
    in_specs = (P(key, None), P(key, "x", None), P(key, "x"))
    out_specs = (P(key), P(key, None))
    return jax.shard_map(local, mesh=fine, in_specs=in_specs, out_specs=out_specs, check_vma=False)
```

```python
import functools

import jax
import jax.numpy as jnp
from jax import lax
from jax.experimental import pallas as pl
from jax.experimental.pallas import tpu as pltpu
from jax.sharding import Mesh, PartitionSpec as P

D = 1024
SLAB = 1024
BR = 16
NBLK = SLAB // BR
NBD = 64
KEYS = 64
NZ, NY, NC, NX = 8, 4, 2, 4
PIECES = NY * NC
RP = BR // PIECES
CX = D // NX
W = RP * CX
PLANE = NX * NY * NC
XBLK = NBLK // NX
LIST = 2 * NBD
TEMP = 0.05

F32, BF16 = jnp.float32, jnp.bfloat16
NT = (((1,), (1,)), ((), ()))
TN = (((0,), (0,)), ((), ()))


def pair_kernel(emb_ref, inc_ref, part_ref, rounded_ref, ownk_ref, cred_ref, credk_ref):
    emb = emb_ref[...]
    quarter = NC * RP * NBD
    group = 2 * quarter
    for first in range(0, NY, 2):
        at = first * quarter
        for n in range(2 * NC * RP):
            y, c, r = first + n // (NC * RP), n // RP % NC, n % RP
            for x in range(NX):
                part_ref[pl.ds(at + n * NBD, NBD), pl.ds(x * CX, CX)] = inc_ref[
                    x, NC * y + c, :, pl.ds(r * CX, CX)
                ]
        part = part_ref[pl.ds(at, group), :]
        cosine = lax.dot_general(part, emb, NT, preferred_element_type=F32)
        weight = jnp.exp((cosine - 1.0) * (1.0 / TEMP))
        rounded = weight.astype(BF16)
        rounded_ref[pl.ds(at, group), :] = rounded
        ownk = jnp.sum(weight, axis=0, keepdims=True)
        if first == 0:
            ownk_ref[...] = ownk
        else:
            ownk_ref[...] += ownk
        credk_ref[pl.ds(at, group), :] = sum(weight[:, n : n + 128] for n in range(0, SLAB, 128))
        cred = jnp.dot(rounded, emb, preferred_element_type=F32).astype(BF16)
        for n in range(2 * NC * RP):
            y, c, r = first + n // (NC * RP), n // RP % NC, n % RP
            for x in range(NX):
                cred_ref[x, NC * y + c, :, pl.ds(r * CX, CX)] = cred[
                    n * NBD : (n + 1) * NBD, x * CX : (x + 1) * CX
                ]


def pair_weights(emb, inc):
    return pl.pallas_call(
        pair_kernel,
        out_shape=(
            pltpu.HBM((SLAB, D), BF16),
            pltpu.HBM((SLAB, SLAB), BF16),
            jax.ShapeDtypeStruct((1, SLAB), F32),
            pltpu.HBM((NX, PIECES, NBD, W), BF16),
            jax.ShapeDtypeStruct((SLAB, 128), F32),
        ),
        compiler_params=pltpu.CompilerParams(vmem_limit_bytes=28 << 20),
        cost_estimate=pl.CostEstimate(
            flops=4 * SLAB * SLAB * D, bytes_accessed=10 << 20, transcendentals=SLAB * SLAB
        ),
    )(emb, inc.reshape(NX, PIECES, NBD, W))


def own_kernel(rounded_ref, part_ref, own_ref):
    own = lax.dot_general(rounded_ref[...], part_ref[...], TN, preferred_element_type=F32)
    own_ref[0] = own.astype(BF16)


def own_sums(rounded, part):
    return pl.pallas_call(
        own_kernel,
        grid=(NX,),
        out_shape=pltpu.HBM((NX, SLAB, CX), BF16),
        in_specs=[
            pl.BlockSpec((SLAB, SLAB), lambda x: (0, 0)),
            pl.BlockSpec((SLAB, CX), lambda x: (0, x)),
        ],
        out_specs=pl.BlockSpec((1, SLAB, CX), lambda x: (x, 0, 0)),
        compiler_params=pltpu.CompilerParams(vmem_limit_bytes=12 << 20),
        cost_estimate=pl.CostEstimate(
            flops=2 * SLAB * SLAB * D, bytes_accessed=6 << 20, transcendentals=0
        ),
    )(*[pltpu.with_memory_space_constraint(a, pltpu.HBM) for a in (rounded, part)])


def shift(axis, by):
    n = lax.axis_size(axis)
    return [(i, (i + by) % n) for i in range(n)]


def up(a, axis):
    return lax.ppermute(a, axis, shift(axis, 1))


def down(a, axis):
    return lax.ppermute(a, axis, shift(axis, -1))


def gather_over_x(mine):
    me = lax.axis_index("x")
    half = SLAB // 2
    parts = [mine[:half], mine[half:]]
    ups = [up(p, "x") for p in parts]
    downs = [down(p, "x") for p in parts]
    far = [up(ups[0], "x"), down(downs[1], "x")]
    place = lambda out, a, row, k: lax.dynamic_update_slice(
        out, a, (row, lax.rem(me + k, NX) * CX)
    )
    out = jnp.concatenate([mine] * NX, axis=1)
    for p in range(2):
        out = place(out, ups[p], p * half, 3)
        out = place(out, downs[p], p * half, 1)
        out = place(out, far[p], p * half, 2)
    return out


def share_in_plane(embeddings, source, block):
    mine = lax.dynamic_slice_in_dim(embeddings, lax.axis_index("x") * (SLAB // NX), SLAB // NX, axis=0)
    rows = jnp.arange(SLAB // NX, dtype=jnp.int32)
    half = PIECES * XBLK
    origin = rows % XBLK * BR + rows % half // XBLK * RP + rows // half
    order = (origin[:, None] == rows[None, :]).astype(BF16)
    mine = jnp.dot(order, mine, preferred_element_type=F32).astype(BF16)
    lists = jnp.broadcast_to(jnp.concatenate([source, block]).astype(BF16), (half, LIST))
    sent = [
        jnp.concatenate([mine[:half, at : at + CX], mine[half:, at : at + CX], lists], axis=1)
        for at in range(0, D, CX)
    ]
    sent = jnp.concatenate(sent).reshape(PLANE, XBLK, W + LIST)
    got = lax.all_to_all(sent, ("x", "y", "c"), 0, 0, tiled=True)
    lists = got[:, 0, W:].astype(jnp.int32)
    source, block = lists[:, :NBD].reshape(-1), lists[:, NBD:].reshape(-1)
    row = ((block // XBLK) * PIECES + source % PIECES) * XBLK + block % XBLK
    return got[:, :, :W].reshape(PLANE * XBLK, W), (source // PIECES) * (PLANE * XBLK) + row


def pick_over_z(held, plane_wanted):
    me = lax.axis_index("z")
    rows = held.shape[0]
    half = rows // 2
    inside = jnp.arange(rows, dtype=jnp.int32)
    picked = None

    def take(picked, parts):
        at = jnp.concatenate(
            [lax.rem(me + k, NZ) * rows + inside[first : first + t.shape[0]] for k, first, t in parts]
        )
        pick = (plane_wanted[:, None] == at[None, :]).astype(BF16)
        got = jnp.dot(pick, jnp.concatenate([t for _, _, t in parts]), preferred_element_type=F32)
        return (got if picked is None else got + picked.astype(F32)).astype(BF16)

    ups = downs = [held[:half], held[half:]]
    picked = take(None, [(0, 0, held)])
    for step in range(1, NZ // 2):
        ups = [up(t, "z") for t in ups]
        downs = [down(t, "z") for t in downs]
        picked = take(
            picked,
            [(NZ - step, p * half, ups[p]) for p in range(2)]
            + [(step, p * half, downs[p]) for p in range(2)],
        )
    far = [(NZ // 2, 0, up(ups[0], "z")), (NZ // 2, half, down(downs[1], "z"))]
    return take(picked, far)


def credit_kernel(targets, first_ref, wanted_ref, back_ref, *refs):
    n_out = len(targets)
    refs, (in_ref, sum_ref, in_sems, out_sems) = refs[:-4], refs[-4:]
    arrived, outs = refs[:-n_out], refs[-n_out:]
    each = len(arrived) // n_out
    rows = outs[0].shape[0]
    loads = [pltpu.make_async_copy(a, in_ref.at[n], in_sems.at[n]) for n, a in enumerate(arrived)]
    stores = [pltpu.make_async_copy(sum_ref.at[i], o, out_sems.at[i]) for i, o in enumerate(outs)]
    for load in loads:
        load.start()
    iota = lax.broadcasted_iota(jnp.int32, (rows, PLANE * NBD), 0)
    spread = jnp.concatenate(
        [
            jnp.where(first_ref[k] + part * rows + iota == wanted_ref[...], 1.0, 0.0).astype(BF16)
            for k, part in targets
        ]
    )
    sums = jnp.dot(spread, back_ref[...], preferred_element_type=F32)
    for i in range(n_out):
        total = sums[i * rows : (i + 1) * rows]
        for n in range(i * each, (i + 1) * each):
            loads[n].wait()
            total += in_ref[n].astype(F32)
        sum_ref[i] = total.astype(BF16)
        stores[i].start()
    for store in stores:
        store.wait()


def credit_sums(targets, first, wanted, back, arrived):
    rows = PIECES * NBLK // 2
    vmem, anywhere = pl.BlockSpec(memory_space=pltpu.VMEM), pl.BlockSpec(memory_space=pl.ANY)
    n_out, n_in = len(targets), max(1, len(arrived))
    return pl.pallas_call(
        functools.partial(credit_kernel, targets),
        out_shape=(jax.ShapeDtypeStruct((rows, W), BF16),) * n_out,
        in_specs=[pl.BlockSpec(memory_space=pltpu.SMEM), vmem, vmem] + [anywhere] * len(arrived),
        out_specs=(anywhere,) * n_out,
        scratch_shapes=[
            pltpu.VMEM((n_in, rows, W), BF16),
            pltpu.VMEM((n_out, rows, W), BF16),
            pltpu.SemaphoreType.DMA((n_in,)),
            pltpu.SemaphoreType.DMA((n_out,)),
        ],
        compiler_params=pltpu.CompilerParams(vmem_limit_bytes=12 << 20),
        cost_estimate=pl.CostEstimate(
            flops=2 * n_out * rows * PLANE * NBD * W, bytes_accessed=3 << 20, transcendentals=0
        ),
    )(first, wanted, back, *arrived)


def exchange_k(plane_k):
    all_k = lax.all_to_all(plane_k.reshape(BR, PIECES, NBLK), ("y", "c"), 1, 0, tiled=True)
    return jnp.sum(all_k.reshape(PIECES, BR, NBLK), axis=0).T.reshape(SLAB)


def first_rows():
    far = lax.axis_index("z") + jnp.arange(NZ, dtype=jnp.int32)
    return lax.rem(far, NZ) * (PIECES * NBLK)


def sum_over_z(back, wanted, first, later):
    def sums(targets, arrived=()):
        return credit_sums(tuple(targets), first, wanted, back, arrived)

    far = NZ // 2
    sent = sums([(far, 0), (far, 1)])
    ups, downs = [up(sent[0], "z"), None], [None, down(sent[1], "z")]
    second = sums([(far - 1, 1), (far + 1, 0)])
    ups[1], downs[0] = up(second[0], "z"), down(second[1], "z")
    third = sums([(far - 1, 0), (far + 1, 1)], [ups[0], downs[1]])
    ups[0], downs[1] = up(third[0], "z"), down(third[1], "z")
    ups[1], later = lax.optimization_barrier((ups[1], later))
    for k in range(far - 2, 0, -1):
        for p in range(2):
            sent = sums([(k, 1 - p), (NZ - k, p)], [ups[1 - p], downs[p]])
            ups[1 - p], downs[p] = up(sent[0], "z"), down(sent[1], "z")
    last = [sums([(0, p)], [ups[p], downs[p]])[0] for p in range(2)]
    return jnp.concatenate(last), later


def local(embeddings, sources, blocks):
    me_x = lax.axis_index("x")
    source, block = sources[0, :, 0], blocks[0]
    held, plane_wanted = share_in_plane(embeddings, source, block)
    outgoing = pick_over_z(held, plane_wanted)
    incoming = lax.all_to_all(outgoing, ("x", "y", "c"), 0, 0, tiled=True)

    part, rounded, own_k, credit, credit_k = pair_weights(embeddings, incoming)
    credit = credit.reshape(PLANE * NBD, W)
    back = lax.all_to_all(credit, ("x", "y", "c"), 0, 0, tiled=True)
    columns = lax.dynamic_slice_in_dim(embeddings, me_x * CX, CX, axis=1)
    wanted, first = plane_wanted[None, :], first_rows()
    back, own, columns, wanted, first = lax.optimization_barrier(
        (back, own_sums(rounded, part), columns, wanted, first)
    )
    own_w = lax.psum_scatter(own, "x", tiled=True)[0]

    per_slot = jnp.sum(credit_k, axis=1).astype(BF16).reshape(BR, NBD)
    every = jnp.arange(KEYS * NBLK, dtype=jnp.int32)
    spread_k = ((source * NBLK + block)[:, None] == every[None, :]).astype(BF16)
    dense_k = jnp.dot(per_slot, spread_k, preferred_element_type=F32)
    dense_k = dense_k.reshape(BR, NZ, PIECES * NBLK).transpose(1, 0, 2)
    plane_k = lax.psum_scatter(dense_k, "z", tiled=True)[0]

    got, plane_k = sum_over_z(back, wanted, first, plane_k)
    got_k = exchange_k(plane_k) + own_k.reshape(SLAB)
    got, own_w, got_k = lax.optimization_barrier((got, own_w, got_k))
    scale = 1.0 + lax.psum(got_k, "x")
    got = got.reshape(NX, PIECES, XBLK, W).transpose(1, 0, 2, 3).reshape(PIECES * NBLK, W)
    got = lax.all_to_all(got, ("y", "c"), 0, 0, tiled=True)
    rows = jnp.arange(SLAB, dtype=jnp.int32)
    origin = (rows % RP) * (SLAB // RP) + (rows % BR) // RP * NBLK + rows // BR
    got = got.reshape(PIECES * NBLK, W)
    got = jnp.concatenate([got[:, r * CX : (r + 1) * CX] for r in range(RP)])
    order = (origin[:, None] == rows[None, :]).astype(BF16)
    total_w = own_w.astype(F32) + jnp.dot(order, got, preferred_element_type=F32)
    mean = ((columns.astype(F32) + total_w) / scale[:, None]).astype(BF16)
    return jnp.log(scale), gather_over_x(lax.optimization_barrier(mean))


def solution(mesh):
    fine = Mesh(mesh.devices.reshape(NZ, NY, NC, NX), ("z", "y", "c", "x"))
    key = ("z", "y", "c")
    in_specs = (P(key, None), P(key, "x", None), P(key, "x"))
    out_specs = (P(key), P(key, None))
    return jax.shard_map(local, mesh=fine, in_specs=in_specs, out_specs=out_specs, check_vma=False)
```

```python
import functools

import jax
import jax.numpy as jnp
from jax import lax
from jax.experimental import pallas as pl
from jax.experimental.pallas import tpu as pltpu
from jax.sharding import Mesh, PartitionSpec as P

D = 1024
SLAB = 1024
BR = 16
NBLK = SLAB // BR
NBD = 64
KEYS = 64
NZ, NY, NC, NX = 8, 4, 2, 4
PIECES = NY * NC
RP = BR // PIECES
CX = D // NX
W = RP * CX
PLANE = NX * NY * NC
XBLK = NBLK // NX
LIST = 2 * NBD
TEMP = 0.05

F32, BF16 = jnp.float32, jnp.bfloat16
NT = (((1,), (1,)), ((), ()))
TN = (((0,), (0,)), ((), ()))


def pair_kernel(emb_ref, inc_ref, part_ref, rounded_ref, ownk_ref, cred_ref, credk_ref):
    emb = emb_ref[...]
    quarter = NC * RP * NBD
    group = 2 * quarter
    for first in range(0, NY, 2):
        at = first * quarter
        for n in range(2 * NC * RP):
            y, c, r = first + n // (NC * RP), n // RP % NC, n % RP
            for x in range(NX):
                part_ref[pl.ds(at + n * NBD, NBD), pl.ds(x * CX, CX)] = inc_ref[
                    x, NC * y + c, :, pl.ds(r * CX, CX)
                ]
        part = part_ref[pl.ds(at, group), :]
        cosine = lax.dot_general(part, emb, NT, preferred_element_type=F32)
        weight = jnp.exp((cosine - 1.0) * (1.0 / TEMP))
        rounded = weight.astype(BF16)
        rounded_ref[pl.ds(at, group), :] = rounded
        ownk = jnp.sum(weight, axis=0, keepdims=True)
        if first == 0:
            ownk_ref[...] = ownk
        else:
            ownk_ref[...] += ownk
        credk_ref[pl.ds(at, group), :] = sum(weight[:, n : n + 128] for n in range(0, SLAB, 128))
        cred = jnp.dot(rounded, emb, preferred_element_type=F32).astype(BF16)
        for n in range(2 * NC * RP):
            y, c, r = first + n // (NC * RP), n // RP % NC, n % RP
            for x in range(NX):
                cred_ref[x, NC * y + c, :, pl.ds(r * CX, CX)] = cred[
                    n * NBD : (n + 1) * NBD, x * CX : (x + 1) * CX
                ]


def pair_weights(emb, inc):
    return pl.pallas_call(
        pair_kernel,
        out_shape=(
            pltpu.HBM((SLAB, D), BF16),
            pltpu.HBM((SLAB, SLAB), BF16),
            jax.ShapeDtypeStruct((1, SLAB), F32),
            pltpu.HBM((NX, PIECES, NBD, W), BF16),
            jax.ShapeDtypeStruct((SLAB, 128), F32),
        ),
        compiler_params=pltpu.CompilerParams(vmem_limit_bytes=28 << 20),
        cost_estimate=pl.CostEstimate(
            flops=4 * SLAB * SLAB * D, bytes_accessed=10 << 20, transcendentals=SLAB * SLAB
        ),
    )(emb, inc.reshape(NX, PIECES, NBD, W))


def own_kernel(rounded_ref, part_ref, own_ref):
    own = lax.dot_general(rounded_ref[...], part_ref[...], TN, preferred_element_type=F32)
    own_ref[0] = own.astype(BF16)


def own_sums(rounded, part):
    return pl.pallas_call(
        own_kernel,
        grid=(NX,),
        out_shape=pltpu.HBM((NX, SLAB, CX), BF16),
        in_specs=[
            pl.BlockSpec((SLAB, SLAB), lambda x: (0, 0)),
            pl.BlockSpec((SLAB, CX), lambda x: (0, x)),
        ],
        out_specs=pl.BlockSpec((1, SLAB, CX), lambda x: (x, 0, 0)),
        compiler_params=pltpu.CompilerParams(vmem_limit_bytes=12 << 20),
        cost_estimate=pl.CostEstimate(
            flops=2 * SLAB * SLAB * D, bytes_accessed=6 << 20, transcendentals=0
        ),
    )(*[pltpu.with_memory_space_constraint(a, pltpu.HBM) for a in (rounded, part)])


def shift(axis, by):
    n = lax.axis_size(axis)
    return [(i, (i + by) % n) for i in range(n)]


def up(a, axis):
    return lax.ppermute(a, axis, shift(axis, 1))


def down(a, axis):
    return lax.ppermute(a, axis, shift(axis, -1))


def gather_over_x(mine):
    me = lax.axis_index("x")
    half = SLAB // 2
    parts = [mine[:half], mine[half:]]
    ups = [up(p, "x") for p in parts]
    downs = [down(p, "x") for p in parts]
    far = [up(ups[0], "x"), down(downs[1], "x")]
    place = lambda out, a, row, k: lax.dynamic_update_slice(
        out, a, (row, lax.rem(me + k, NX) * CX)
    )
    out = jnp.concatenate([mine] * NX, axis=1)
    for p in range(2):
        out = place(out, ups[p], p * half, 3)
        out = place(out, downs[p], p * half, 1)
        out = place(out, far[p], p * half, 2)
    return out


def share_in_plane(embeddings, source, block):
    mine = lax.dynamic_slice_in_dim(embeddings, lax.axis_index("x") * (SLAB // NX), SLAB // NX, axis=0)
    rows = jnp.arange(SLAB // NX, dtype=jnp.int32)
    half = PIECES * XBLK
    origin = rows % XBLK * BR + rows % half // XBLK * RP + rows // half
    order = (origin[:, None] == rows[None, :]).astype(BF16)
    mine = jnp.dot(order, mine, preferred_element_type=F32).astype(BF16)
    lists = jnp.broadcast_to(jnp.concatenate([source, block]).astype(BF16), (half, LIST))
    sent = [
        jnp.concatenate([mine[:half, at : at + CX], mine[half:, at : at + CX], lists], axis=1)
        for at in range(0, D, CX)
    ]
    sent = jnp.concatenate(sent).reshape(PLANE, XBLK, W + LIST)
    got = lax.all_to_all(sent, ("x", "y", "c"), 0, 0, tiled=True)
    lists = got[:, 0, W:].astype(jnp.int32)
    source, block = lists[:, :NBD].reshape(-1), lists[:, NBD:].reshape(-1)
    row = ((block // XBLK) * PIECES + source % PIECES) * XBLK + block % XBLK
    return got[:, :, :W].reshape(PLANE * XBLK, W), (source // PIECES) * (PLANE * XBLK) + row


def pick_over_z(held, plane_wanted):
    me = lax.axis_index("z")
    rows = held.shape[0]
    half = rows // 2
    inside = jnp.arange(rows, dtype=jnp.int32)
    picked = None

    def take(picked, parts):
        at = jnp.concatenate(
            [lax.rem(me + k, NZ) * rows + inside[first : first + t.shape[0]] for k, first, t in parts]
        )
        pick = (plane_wanted[:, None] == at[None, :]).astype(BF16)
        got = jnp.dot(pick, jnp.concatenate([t for _, _, t in parts]), preferred_element_type=F32)
        return (got if picked is None else got + picked.astype(F32)).astype(BF16)

    ups = downs = [held[:half], held[half:]]
    picked = take(None, [(0, 0, held)])
    for step in range(1, NZ // 2):
        ups = [up(t, "z") for t in ups]
        downs = [down(t, "z") for t in downs]
        picked = take(
            picked,
            [(NZ - step, p * half, ups[p]) for p in range(2)]
            + [(step, p * half, downs[p]) for p in range(2)],
        )
    far = [(NZ // 2, 0, up(ups[0], "z")), (NZ // 2, half, down(downs[1], "z"))]
    return take(picked, far)


def credit_kernel(targets, first_ref, wanted_ref, back_ref, *refs):
    n_out = len(targets)
    refs, (in_ref, sum_ref, in_sems, out_sems) = refs[:-4], refs[-4:]
    arrived, outs = refs[:-n_out], refs[-n_out:]
    each = len(arrived) // n_out
    rows = outs[0].shape[0]
    loads = [pltpu.make_async_copy(a, in_ref.at[n], in_sems.at[n]) for n, a in enumerate(arrived)]
    stores = [pltpu.make_async_copy(sum_ref.at[i], o, out_sems.at[i]) for i, o in enumerate(outs)]
    for load in loads:
        load.start()
    iota = lax.broadcasted_iota(jnp.int32, (rows, PLANE * NBD), 0)
    for i, (k, part) in enumerate(targets):
        row = first_ref[k] + part * rows + iota
        spread = jnp.where(row == wanted_ref[...], 1.0, 0.0).astype(BF16)
        total = jnp.dot(spread, back_ref[...], preferred_element_type=F32)
        for n in range(i * each, (i + 1) * each):
            loads[n].wait()
            total += in_ref[n].astype(F32)
        sum_ref[i] = total.astype(BF16)
        stores[i].start()
    for store in stores:
        store.wait()


def credit_sums(targets, first, wanted, back, arrived):
    rows = PIECES * NBLK // 2
    vmem, anywhere = pl.BlockSpec(memory_space=pltpu.VMEM), pl.BlockSpec(memory_space=pl.ANY)
    n_out, n_in = len(targets), max(1, len(arrived))
    return pl.pallas_call(
        functools.partial(credit_kernel, targets),
        out_shape=(jax.ShapeDtypeStruct((rows, W), BF16),) * n_out,
        in_specs=[pl.BlockSpec(memory_space=pltpu.SMEM), vmem, vmem] + [anywhere] * len(arrived),
        out_specs=(anywhere,) * n_out,
        scratch_shapes=[
            pltpu.VMEM((n_in, rows, W), BF16),
            pltpu.VMEM((n_out, rows, W), BF16),
            pltpu.SemaphoreType.DMA((n_in,)),
            pltpu.SemaphoreType.DMA((n_out,)),
        ],
        compiler_params=pltpu.CompilerParams(vmem_limit_bytes=12 << 20),
        cost_estimate=pl.CostEstimate(
            flops=2 * n_out * rows * PLANE * NBD * W, bytes_accessed=3 << 20, transcendentals=0
        ),
    )(first, wanted, back, *arrived)


def exchange_k(plane_k):
    all_k = lax.all_to_all(plane_k.reshape(BR, PIECES, NBLK), ("y", "c"), 1, 0, tiled=True)
    return jnp.sum(all_k.reshape(PIECES, BR, NBLK), axis=0).T.reshape(SLAB)


def first_rows():
    far = lax.axis_index("z") + jnp.arange(NZ, dtype=jnp.int32)
    return lax.rem(far, NZ) * (PIECES * NBLK)


def sum_over_z(back, wanted, first, later):
    def sums(targets, arrived=()):
        return credit_sums(tuple(targets), first, wanted, back, arrived)

    far = NZ // 2
    sent = sums([(far, 0), (far, 1)])
    ups, downs = [up(sent[0], "z"), None], [None, down(sent[1], "z")]
    second = sums([(far - 1, 1), (far + 1, 0)])
    ups[1], downs[0] = up(second[0], "z"), down(second[1], "z")
    third = sums([(far - 1, 0), (far + 1, 1)], [ups[0], downs[1]])
    ups[0], downs[1] = up(third[0], "z"), down(third[1], "z")
    ups[1], later = lax.optimization_barrier((ups[1], later))
    for k in range(far - 2, 0, -1):
        for p in range(2):
            sent = sums([(k, 1 - p), (NZ - k, p)], [ups[1 - p], downs[p]])
            ups[1 - p], downs[p] = up(sent[0], "z"), down(sent[1], "z")
    last = [sums([(0, p)], [ups[p], downs[p]])[0] for p in range(2)]
    return jnp.concatenate(last), later


def local(embeddings, sources, blocks):
    me_x = lax.axis_index("x")
    source, block = sources[0, :, 0], blocks[0]
    held, plane_wanted = share_in_plane(embeddings, source, block)
    outgoing = pick_over_z(held, plane_wanted)
    incoming = lax.all_to_all(outgoing, ("x", "y", "c"), 0, 0, tiled=True)

    part, rounded, own_k, credit, credit_k = pair_weights(embeddings, incoming)
    credit = credit.reshape(PLANE * NBD, W)
    back = lax.all_to_all(credit, ("x", "y", "c"), 0, 0, tiled=True)
    columns = lax.dynamic_slice_in_dim(embeddings, me_x * CX, CX, axis=1)
    wanted, first = plane_wanted[None, :], first_rows()
    back, own, columns, wanted, first = lax.optimization_barrier(
        (back, own_sums(rounded, part), columns, wanted, first)
    )
    own_w = lax.psum_scatter(own, "x", tiled=True)[0]

    per_slot = jnp.sum(credit_k, axis=1).astype(BF16).reshape(BR, NBD)
    every = jnp.arange(KEYS * NBLK, dtype=jnp.int32)
    spread_k = ((source * NBLK + block)[:, None] == every[None, :]).astype(BF16)
    dense_k = jnp.dot(per_slot, spread_k, preferred_element_type=F32)
    dense_k = dense_k.reshape(BR, NZ, PIECES * NBLK).transpose(1, 0, 2)
    plane_k = lax.psum_scatter(dense_k, "z", tiled=True)[0]

    got, plane_k = sum_over_z(back, wanted, first, plane_k)
    got_k = exchange_k(plane_k) + own_k.reshape(SLAB)
    got, own_w, got_k = lax.optimization_barrier((got, own_w, got_k))
    scale = 1.0 + lax.psum(got_k, "x")
    got = got.reshape(NX, PIECES, XBLK, W).transpose(1, 0, 2, 3).reshape(PIECES * NBLK, W)
    got = lax.all_to_all(got, ("y", "c"), 0, 0, tiled=True)
    rows = jnp.arange(SLAB, dtype=jnp.int32)
    origin = (rows % RP) * (SLAB // RP) + (rows % BR) // RP * NBLK + rows // BR
    got = got.reshape(PIECES * NBLK, W)
    got = jnp.concatenate([got[:, r * CX : (r + 1) * CX] for r in range(RP)])
    order = (origin[:, None] == rows[None, :]).astype(BF16)
    total_w = own_w.astype(F32) + jnp.dot(order, got, preferred_element_type=F32)
    mean = ((columns.astype(F32) + total_w) / scale[:, None]).astype(BF16)
    return jnp.log(scale), gather_over_x(lax.optimization_barrier(mean))


def solution(mesh):
    fine = Mesh(mesh.devices.reshape(NZ, NY, NC, NX), ("z", "y", "c", "x"))
    key = ("z", "y", "c")
    in_specs = (P(key, None), P(key, "x", None), P(key, "x"))
    out_specs = (P(key), P(key, None))
    return jax.shard_map(local, mesh=fine, in_specs=in_specs, out_specs=out_specs, check_vma=False)
```
